32 devices in a mesh: row: 16 (over z, x, core), col: 2 (over y).
Axes of the slice: x: 2, y: 2, z: 4, core: 2. Of those that a mesh axis runs over, the one named last changes fastest.
Arguments:
- sigma_anc: float32 [48, 48, 128, 128], P('row', 'col'), as said below
- factor: float32 [16, 32, 128, 128], P('row', 'col'), may hold values from -1.25 to 1.25
- diag_inv: float32 [32, 128, 128], P('col'), as said below
- struct: int32 [32, 16], P('col'), may hold values from 0 to 47, all different within a row
Outputs:
- z_off: float32 [32, 48, 128, 128], P('col', 'row')
- z_diag: float32 [32, 128, 128], P(('col', 'row'))
The draws below stay inside these ranges and needn't reach their ends.
Inputs may be any that keep to these rules, and one draw needn't show every extreme that they name: Each row of struct names 16 different ancestor blocks, and every ancestor block is named by some row. sigma_anc is symmetric: block [b, a] is the transpose of block [a, b]. Each diag_inv[k] is lower triangular with a positive diagonal.
All inputs are finite; a program needn't handle non-finite values.
Results may differ from the reference program's by a relative error of at most 0.0003.
Values sent between devices are 32-bit elements; how exact they have to be, the bound alone decides.
No kernel may reach another device: no remote copies, remote signals or barrier semaphores. Data moves between devices by JAX's collectives and lax.ppermute only.
A program may use at most 128 MiB of HBM per device.

```python
from functools import partial
import jax
import jax.numpy as jnp
from jax import lax

B = 128
S = 16
NA = 48
NK = 32


def draw_sigma_anc(key, part):
    first_key, second_key = jax.random.split(jax.random.fold_in(key, 11))
    noise = jax.random.normal(first_key, (NA, NA, B, B), jnp.float32)
    level = jax.random.uniform(second_key, (NA, B), jnp.float32, 1.0, 2.0)
    scale = (NA * B) ** (-0.5)
    mirrored = (noise + jnp.transpose(noise, (1, 0, 3, 2))) * (scale * 0.7071067811865476)
    blocks = jnp.arange(NA)
    cells = jnp.arange(B)
    same_block = blocks[:, None, None, None] == blocks[None, :, None, None]
    same_cell = cells[None, None, :, None] == cells[None, None, None, :]
    return mirrored + jnp.where(same_block & same_cell, level[:, None, :, None], 0.0)


def draw_diag_inv(key, part):
    first_key, second_key = jax.random.split(jax.random.fold_in(key, 23))
    lower = jnp.clip(jax.random.normal(first_key, (NK, B, B), jnp.float32), -4.0, 4.0)
    middle = jax.random.uniform(second_key, (NK, B), jnp.float32, 0.5, 1.5)
    cells = jnp.arange(B)
    below = cells[:, None] > cells[None, :]
    on_diag = cells[:, None] == cells[None, :]
    strict = jnp.where(below[None, :, :], lower * (0.5 * B ** (-0.5)), 0.0)
    return strict + jnp.where(on_diag[None, :, :], middle[:, :, None], 0.0)


def block_levels(own_key, dims, cuts, least, largest):
    loudness, own = 1.0, jax.random.fold_in(own_key, 6)
    for position, parts in cuts:
        heights = jnp.exp(jax.random.uniform(jax.random.fold_in(own, position), (parts,), jnp.float32, least / len(cuts), largest / len(cuts)))
        loudness = loudness * jnp.repeat(heights, dims[position] // parts).reshape([-1 if axis == position else 1 for axis in range(len(dims))])
    return loudness


def picks_of(rng, rows, amount, top, lift):
    sequence = jax.random.permutation(jax.random.fold_in(rng, 1), amount)
    favour = sequence
    for power in range(3):
        favour = favour * favour // amount
    favour = favour * lift // amount
    lots = jax.random.randint(jax.random.fold_in(rng, 2), (rows, amount), 0, 4096) + favour
    sure = jax.random.permutation(jax.random.fold_in(rng, 3), rows)[jnp.arange(amount) % rows]
    lots = jnp.where(jnp.arange(rows)[:, None] == sure[None, :], 1 << 14, lots)
    priority = lots * amount + jnp.arange(amount)
    return lax.top_k(priority.astype(jnp.int32), top)[1].astype(jnp.int32)


def bell_draw(stream_key, shape, deviation, limit, cuts=(), held_as=jnp.bfloat16):
    array = jax.random.normal(stream_key, shape, jnp.float32) * deviation
    if len(cuts) > 0:
        array = block_levels(stream_key, shape, cuts, -0.22, 0.18) * array
    return jnp.clip(array, min=-limit, max=limit).astype(held_as)


def setup_inputs(seed: int = 0) -> dict:
    key_of = jax.random.split(jax.random.key(seed), 5)
    sigma_anc = draw_sigma_anc(jax.random.fold_in(key_of[4], 71), 0)
    factor = bell_draw(key_of[1], (S, NK, B, B), 0.2, 1.25, ((0, 16), (1, 2)), jnp.float32)
    diag_inv = draw_diag_inv(jax.random.fold_in(key_of[4], 71), 0)
    struct = picks_of(key_of[3], NK, NA, S, 2730)
    return dict(sigma_anc=sigma_anc, factor=factor, diag_inv=diag_inv, struct=struct)


highest = lax.Precision.HIGHEST


def one_node(sigma_anc, element):
    factor_node, slot_ids, inverse_node = element
    u_node = jnp.einsum("sij,jl->sil", factor_node, inverse_node, precision=highest)
    picked = jnp.take(sigma_anc, slot_ids, axis=1)
    y_node = jnp.einsum("asij,sjl->ail", picked, u_node, precision=highest)
    ancestors = jnp.arange(sigma_anc.shape[0], dtype=jnp.int32)
    member = jnp.any(slot_ids[:, None] == ancestors[None, :], axis=0)
    z_block = jnp.where(member[:, None, None], -y_node, 0.0)
    y_slots = jnp.take(y_node, slot_ids, axis=0)
    inverse_part = jnp.einsum("ij,il->jl", inverse_node, inverse_node, precision=highest)
    z_middle = inverse_part + jnp.einsum("sij,sil->jl", u_node, y_slots, precision=highest)
    return z_block, z_middle


def reference(sigma_anc, factor, diag_inv, struct):
    z_off, z_diag = lax.map(partial(one_node, sigma_anc), (jnp.moveaxis(factor, 1, 0), struct, diag_inv))
    return z_off, z_diag
```

```python
import functools

import jax
import jax.numpy as jnp
import numpy as np
from jax import lax
from jax.experimental import pallas as pl
from jax.experimental.pallas import tpu as pltpu
from jax.sharding import PartitionSpec as P

F32 = jnp.float32
BF16 = jnp.bfloat16
I32 = jnp.int32
MIB = 1024 * 1024
VMEM = pltpu.VMEM
SMEM = pltpu.SMEM
UNROLL = 4


def split(x):
    hi = x.astype(BF16)
    return hi, (x - hi.astype(F32)).astype(BF16)


def wide(x):
    hi, lo = split(x)
    return jnp.concatenate([hi, lo], axis=-1)


def tall(x):
    both = wide(x)
    return jnp.concatenate([both, both], axis=-2)


def fold(product):
    half = product.shape[-1] // 2
    return product[..., :half] + product[..., half:]


def dot(left, right):
    return jnp.dot(left, right, preferred_element_type=F32)


def dot_t(left, right):
    stacked = jnp.concatenate(split(left), axis=0)
    return fold(
        lax.dot_general(stacked, tall(right), (((0,), (0,)), ((), ())), preferred_element_type=F32)
    )


def u_kernel(nodes, factor, inverse, token, own, other):
    del token
    count = own.shape[0]
    for t in range(count):
        for w, out in ((0, own), (1, other)):
            n = nodes[w * count + t]
            out[t] = fold(dot(wide(factor[n]), tall(inverse[n])))


def u_chunk(nodes, factor, inverse, token, count):
    shape = jax.ShapeDtypeStruct((count,) + inverse.shape[1:], F32)
    return pl.pallas_call(
        u_kernel,
        out_shape=(shape, shape),
        in_specs=[
            pl.BlockSpec(memory_space=SMEM),
            pl.BlockSpec(memory_space=VMEM),
            pl.BlockSpec(memory_space=VMEM),
            pl.BlockSpec(memory_space=pl.ANY),
        ],
        out_specs=(pl.BlockSpec(memory_space=VMEM),) * 2,
        compiler_params=pltpu.CompilerParams(vmem_limit_bytes=16 * MIB),
        name="u_chunk",
    )(nodes, factor, inverse, token)


def halves_kernel(own, partner, out):
    def step(b, carry):
        out[0, 0, b] = wide(own[0, b])
        out[1, 0, b] = wide(partner[0, b])
        return carry

    lax.fori_loop(0, own.shape[1], step, 0)


def sigma_halves(own, partner):
    rows, cols, width, _ = own.shape
    spec = pl.BlockSpec((1, cols, width, width), lambda i: (i, 0, 0, 0))
    return pl.pallas_call(
        halves_kernel,
        grid=(rows,),
        out_shape=jax.ShapeDtypeStruct((2, rows, cols, width, 2 * width), BF16),
        in_specs=[spec, spec],
        out_specs=pl.BlockSpec((2, 1, cols, width, 2 * width), lambda i: (0, i, 0, 0, 0)),
        compiler_params=pltpu.CompilerParams(vmem_limit_bytes=24 * MIB),
        name="sigma_halves",
    )(own, partner)


def early_kernel(dims, perm, pos_of, class_of, slot_of, *refs):
    rows, cols, pieces, half = dims
    hl_local, first_own, first_part, rest_own, rest_part = refs[:5]
    plain = refs[5 : 5 + pieces - 2]
    far = refs[5 + pieces - 2 : 5 + pieces + 2]
    y_own, y_part, p_out, u_out = refs[5 + pieces + 2 : 9 + pieces + 2]
    hl, first_buf, rest_buf, acc, sems = refs[9 + pieces + 2 :]
    t = pl.program_id(0)
    width = p_out.shape[-1]
    groups = first_own.shape[0]

    @pl.when(t == 0)
    def prologue():
        copies = []
        for w, (first, rest) in enumerate(((first_own, rest_own), (first_part, rest_part))):
            copies.append(pltpu.make_async_copy(first, first_buf.at[w], sems.at[2 * w]))
            copies.append(pltpu.make_async_copy(rest, rest_buf.at[w], sems.at[2 * w + 1]))
        local = pltpu.make_async_copy(hl_local, hl.at[:, pl.ds(0, cols)], sems.at[4])
        for copy in copies:
            copy.start()
        local.start()

        def clear(m, carry):
            for w in range(2):
                for i in range(rows):
                    for c in range(i):
                        hl[w * rows + i, cols + m * rows + c] = jnp.zeros((width, 2 * width), BF16)
            return carry

        lax.fori_loop(0, groups, clear, 0)
        for w in range(2):
            copies[2 * w].wait()
            copies[2 * w + 1].wait()

            def spread(m, carry):
                for c in range(rows):
                    hl[w * rows, cols + m * rows + c] = wide(first_buf[w, m, c])
                pair = 0
                for i in range(1, rows):
                    for c in range(i, rows):
                        hl[w * rows + i, cols + m * rows + c] = wide(rest_buf[w, m, pair])
                        pair += 1
                return carry

            lax.fori_loop(0, groups, spread, 0)
        local.wait()

    acc[...] = jnp.zeros_like(acc)
    near = perm[t] < half
    place = 0
    for j in range(pieces):
        if j % (pieces // 2) == pieces // 2 - 1:
            which = 2 * (j // (pieces // 2))
            u = jnp.where(near, far[which][0], far[which + 1][0])
        else:
            u = plain[place][0]
            place += 1
        u_out[0, j] = u
        left = hl[:, pos_of[t * pieces + j]].reshape(2 * rows * width, 2 * width)
        acc[class_of[t * pieces + j]] += fold(dot(left, tall(u)))

    total = jnp.zeros((width, width), F32)
    for w, out in enumerate((y_own, y_part)):
        for i in range(rows):
            at = pl.ds((w * rows + i) * width, width)
            parts = [acc[c, at] for c in range(rows)]
            out[0, i] = sum(parts[1:], parts[0])
            later = parts[i]
            for c in range(i + 1, rows):
                later = later + 2.0 * parts[c]
            slot = slot_of[t * 2 * rows + w * rows + i]
            later = jnp.where(slot >= 0, later, 0.0)
            total = total + dot_t(u_out[0, jnp.maximum(slot, 0)], later)
    p_out[0] = 0.5 * (total + total.T)


def early_sums(perm, pos_of, class_of, slot_of, hl_local, firsts, rests, plain, far, window):
    count, width = plain[0].shape[0], plain[0].shape[-1]
    pieces = len(plain) + 2
    rows2, cols = hl_local.shape[:2]
    rows = rows2 // 2
    half = count // 2
    groups = firsts[0].shape[0]
    any_spec = pl.BlockSpec(memory_space=pl.ANY)

    def node(t, perm, *_):
        return (perm[t], 0, 0)

    def low(t, perm, *_):
        return (jnp.minimum(perm[t], half - 1), 0, 0)

    def high(t, perm, *_):
        return (jnp.maximum(perm[t] - half, 0), 0, 0)

    block = (1, width, width)
    y_spec = pl.BlockSpec((1, rows, width, width), lambda t, perm, *_: (perm[t], 0, 0, 0))
    y_shape = jax.ShapeDtypeStruct((count, rows, width, width), F32)
    return pl.pallas_call(
        functools.partial(early_kernel, (rows, cols, pieces, half)),
        grid_spec=pltpu.PrefetchScalarGridSpec(
            num_scalar_prefetch=4,
            grid=(count,),
            in_specs=[any_spec] * 5
            + [pl.BlockSpec(block, node)] * len(plain)
            + [pl.BlockSpec(block, low), pl.BlockSpec(block, high)] * 2,
            out_specs=(
                y_spec,
                y_spec,
                pl.BlockSpec(block, lambda t, *_: (t, 0, 0)),
                pl.BlockSpec((1, pieces, width, width), lambda t, perm, *_: (perm[t], 0, 0, 0)),
            ),
            scratch_shapes=[
                pltpu.VMEM((rows2, window, width, 2 * width), BF16),
                pltpu.VMEM((2,) + firsts[0].shape, F32),
                pltpu.VMEM((2,) + rests[0].shape, F32),
                pltpu.VMEM((rows, rows2 * width, width), F32),
                pltpu.SemaphoreType.DMA((5,)),
            ],
        ),
        out_shape=(
            y_shape,
            y_shape,
            jax.ShapeDtypeStruct((count, width, width), F32),
            jax.ShapeDtypeStruct((count, pieces, width, width), F32),
        ),
        compiler_params=pltpu.CompilerParams(vmem_limit_bytes=44 * MIB),
        name="early_sums",
    )(perm, pos_of, class_of, slot_of, hl_local, firsts[0], firsts[1], rests[0], rests[1], *plain, *far)


def late_kernel(dims, items, bounds, place_of, node_of, member, *refs):
    first_row, rows, pieces, fresh = dims
    late = refs[0]
    u_sets = refs[1:5]
    if fresh:
        y_sets, (out, z, hl, u_buf, sems) = refs[5:9], refs[9:]
    else:
        source, (out, z, hl, u_buf, sems) = refs[5], refs[6:]
    groups, span, width, _ = late.shape
    per_set = u_sets[0].shape[0]
    total = bounds[4]

    def u_copy(a, index, item):
        return pltpu.make_async_copy(
            u_sets[a].at[lax.rem(lax.div(item, pieces), per_set), lax.rem(item, pieces)], u_buf.at[index], sems.at[0]
        )

    for a in range(4):

        def fetch(index, carry):
            u_copy(a, index, items[index]).start()
            return carry

        lax.fori_loop(bounds[a], bounds[a + 1], fetch, 0)
    base = rows - span
    if fresh:
        copies = [
            pltpu.make_async_copy(y_sets[a].at[t], z.at[node_of[a * per_set + t]], sems.at[1])
            for a in range(4)
            for t in range(per_set)
        ]
    else:
        copies = [pltpu.make_async_copy(source.at[:, pl.ds(base, span)], z, sems.at[1])]
    for copy in copies:
        copy.start()

    def spread(m, carry):
        for i in range(span):
            hl[m, i] = wide(late[m, i])
        return carry

    lax.fori_loop(0, groups, spread, 0)
    hl[groups] = jnp.zeros((span, width, 2 * width), BF16)
    for copy in copies:
        copy.wait()

    def arrive(index, carry):
        u_copy(0, index, items[0]).wait()
        return carry

    lax.fori_loop(0, total, arrive, 0)

    def work(step, carry):
        products = []
        for v in range(UNROLL):
            index = step * UNROLL + v
            valid = index < total
            index = jnp.minimum(index, total - 1)
            item = items[index]
            spot = jnp.where(valid, place_of[item], groups)
            left = hl[spot].reshape(span * width, 2 * width)
            products.append((node_of[lax.div(item, pieces)], fold(dot(left, tall(u_buf[index])))))
        for n, product in products:
            for i in range(span):
                part = product[i * width : (i + 1) * width]
                if fresh:
                    z[n, base + i] += part
                else:
                    z[n, i] -= jnp.where(member[n * rows + base + i] > 0, part, 0.0)
        return carry

    lax.fori_loop(0, lax.div(total + UNROLL - 1, UNROLL), work, 0)
    if fresh:

        def finish(n, carry):
            for i in range(rows):
                z[n, i] = jnp.where(member[n * rows + i] > 0, -z[n, i], 0.0)
            return carry

        lax.fori_loop(0, z.shape[0], finish, 0)
        back = pltpu.make_async_copy(z, out, sems.at[1])
    else:
        back = pltpu.make_async_copy(z, out.at[:, pl.ds(base, span)], sems.at[1])
    back.start()
    back.wait()


def late_sums(tables, late, u_sets, y_sets, z_before, shape, pieces):
    items, bounds, place_of, node_of, member = tables
    nodes, rows, width, _ = shape
    groups, span = late.shape[:2]
    fresh = z_before is None
    any_spec = pl.BlockSpec(memory_space=pl.ANY)
    operands = list(u_sets) + (list(y_sets) if fresh else [z_before])
    return pl.pallas_call(
        functools.partial(late_kernel, (rows - span, rows, pieces, fresh)),
        in_specs=[pl.BlockSpec(memory_space=SMEM)] * 5 + [pl.BlockSpec(memory_space=VMEM)] + [any_spec] * len(operands),
        out_specs=any_spec,
        out_shape=jax.ShapeDtypeStruct(shape, F32),
        scratch_shapes=[
            pltpu.VMEM((nodes, rows if fresh else span, width, width), F32),
            pltpu.VMEM((groups + 1, span, width, 2 * width), BF16),
            pltpu.VMEM((items.shape[0], width, width), F32),
            pltpu.SemaphoreType.DMA((2,)),
        ],
        input_output_aliases={} if fresh else {10: 0},
        compiler_params=pltpu.CompilerParams(vmem_limit_bytes=40 * MIB),
        name="late_sums",
    )(items, bounds, place_of, node_of, member, late, *operands)


def ring_order(chips):
    return list(range(0, chips, 2)) + list(range(1, chips, 2))[::-1]


def body(n_row, n_col, sigma, factor, diag_inv, struct):
    rows, cols, width, _ = sigma.shape
    nodes = diag_inv.shape[0]
    window = cols * n_col
    chips = n_row // 2
    order = ring_order(chips)
    zs = chips // 2
    row = lax.axis_index("row")
    col = lax.axis_index("col")
    chip, core = row // 2, row % 2
    my_z, my_x = chip // 2, chip % 2
    permute = lax.ppermute

    def pairs(step):
        return [(order[i] * 2 + c, order[(i + step) % chips] * 2 + c) for i in range(chips) for c in range(2)]

    swap_core = [(r, r ^ 1) for r in range(n_row)]
    swap_x = [(r, r ^ 2) for r in range(n_row)]
    full_hops = (chips - 1) // 2

    table = np.zeros((n_row, n_row), np.int32)
    for r in range(n_row):
        p = order.index(r // 2)
        hops = [0] + [-h for h in range(1, full_hops + 1)] + list(range(1, full_hops + 1)) + [chips // 2]
        for w in range(2):
            for j, h in enumerate(hops):
                table[r, w * chips + j] = 2 * order[(p + h) % chips] + ((r % 2) ^ w)
    pieces = n_row
    node_ids = jnp.arange(nodes, dtype=I32)
    slots = jnp.asarray(table)[2 * chip + node_ids % 2]
    blocks = jnp.take_along_axis(struct, slots, axis=1)
    shift = (blocks // cols - col) % n_col
    pos_all = shift * cols + blocks % cols
    class_all = blocks % rows
    row_ids = jnp.arange(rows, dtype=I32)
    my_rows = jnp.concatenate([row * rows + row_ids, (row ^ 1) * rows + row_ids])
    hit = blocks[:, :, None] == my_rows[None, None, :]
    is_member = jnp.any(hit, axis=1)
    slot_all = jnp.where(is_member, jnp.argmax(hit, axis=1), -1).astype(I32)

    chunk_z = [[0, zs - 1], list(range(1, zs - 1))] if zs == 4 else [[z] for z in range(zs)]
    chunk_gn = [[2 * z + x for z in zz for x in range(2)] for zz in chunk_z]

    groups = sigma.reshape(rows, cols // rows, rows, width, width)

    def part(which):
        return jnp.stack([groups[i, :, c] for i, c in which], axis=1)

    def over_col(source):
        got = [permute(source, "col", [((c + d) % n_col, c) for c in range(n_col)]) for d in range(1, n_col)]
        return got[0] if len(got) == 1 else jnp.concatenate(got, axis=0)

    first_own = over_col(part([(0, c) for c in range(rows)]))
    rest_own = over_col(part([(i, c) for i in range(1, rows) for c in range(i, rows)]))
    late_parts = []
    token = first_own
    for c in range(rows - 1):
        source = part([(i, c) for i in range(c + 1, rows)])
        source, token = lax.optimization_barrier((source, token))
        late_parts.append(over_col(source))
        token = rest_own
    sigma_part = permute(sigma, "row", swap_core)
    hl_local = sigma_halves(sigma, sigma_part).reshape(2 * rows, cols, width, 2 * width)
    first_part = permute(first_own, "row", swap_core)
    rest_part = permute(rest_own, "row", swap_core)

    def ring(u):
        half = u.shape[0] // 2
        right, left = [u], [u]
        for _ in range(full_hops):
            right.append(permute(right[-1], "row", pairs(1)))
            left.append(permute(left[-1], "row", pairs(-1)))
        far = [permute(right[-1][:half], "row", pairs(1)), permute(left[-1][half:], "row", pairs(-1))]
        return right, left, far

    token = struct
    y_own, y_part, u_own, sums = [], [], [], []
    for zz, gn in zip(chunk_z, chunk_gn):
        count = len(gn)
        gn_ids = jnp.asarray(gn, I32)
        mine = 2 * gn_ids + core
        ids = jnp.concatenate([mine, 2 * gn_ids + 1 - core])
        u_mine, u_theirs = u_chunk(ids, factor[0], diag_inv, token, count)
        u_partner = permute(u_theirs, "row", swap_core)
        plain, far = [], []
        for u in (u_mine, u_partner):
            right, left, ends = ring(u)
            plain += right + left[1:]
            far += ends
            token = right[2]
        perm = jnp.concatenate([jnp.arange(0, count, 2, dtype=I32) + my_x, jnp.arange(0, count, 2, dtype=I32) + 1 - my_x])
        turn = mine[perm]
        y_a, y_b, p_sum, u_all = early_sums(
            perm,
            pos_all[turn].reshape(-1),
            class_all[turn].reshape(-1),
            slot_all[turn].reshape(-1),
            hl_local,
            (first_own, first_part),
            (rest_own, rest_part),
            plain,
            far,
            window,
        )
        y_own.append(y_a)
        y_part.append(permute(y_b, "row", swap_core))
        u_own.append(u_all)
        half = count // 2
        sums.append(p_sum[:half] + permute(p_sum[half:], "row", swap_x))
    u_part = [permute(u, "row", swap_core) for u in u_own]

    share = lax.dynamic_slice_in_dim(diag_inv, row, 1, 0)
    z_diag = jnp.einsum("kij,kil->kjl", share, share, precision=lax.Precision.HIGHEST)
    for zz, part_sum in zip(chunk_z, sums):
        for i, z in enumerate(zz):
            z_diag = z_diag + jnp.where(my_z == z, part_sum[i], 0.0)[None]
        for m in range(1, zs):
            send = part_sum[0]
            links = []
            for i, z in enumerate(zz):
                from_z = (z + m) % zs
                send = jnp.where(my_z == from_z, part_sum[i], send)
                links += [(from_z * 4 + low, z * 4 + low) for low in range(4)]
            z_diag = z_diag + permute(send, "row", links)[None]

    in_sets = jnp.concatenate(
        [2 * jnp.asarray(gn, I32) + core for gn in chunk_gn] + [2 * jnp.asarray(gn, I32) + 1 - core for gn in chunk_gn]
    )
    member = is_member[:, :rows]
    place = (((pos_all - cols) // rows)[in_sets]).reshape(-1).astype(I32)
    z_off = None
    u_sets = u_own + u_part
    for c, late in enumerate(late_parts):
        wanted = (shift > 0) & (class_all == c) & jnp.any(member[:, c + 1 :], axis=1)[:, None]
        wanted = wanted[in_sets].reshape(-1)
        total = wanted.shape[0]
        index = jnp.arange(total, dtype=I32)
        items = jnp.sort(jnp.where(wanted, index, total + index))
        ends = jnp.cumsum(jnp.sum(wanted.reshape(4, -1), axis=1))
        bounds = jnp.concatenate([jnp.zeros((1,), I32), ends.astype(I32)])
        tables = (items, bounds, place, in_sets, member.reshape(-1).astype(I32))
        z_off = late_sums(tables, late, u_sets, y_own + y_part, z_off, (nodes, rows, width, width), pieces)
    return z_off, z_diag


def solution(mesh):
    in_specs = (
        P("row", "col", None, None),
        P("row", "col", None, None),
        P("col", None, None),
        P("col", None),
    )
    out_specs = (P("col", "row", None, None), P(("col", "row"), None, None))
    run = functools.partial(body, mesh.shape["row"], mesh.shape["col"])
    return jax.shard_map(run, mesh=mesh, in_specs=in_specs, out_specs=out_specs, check_vma=False)
```

```python
import functools

import jax
import jax.numpy as jnp
import numpy as np
from jax import lax
from jax.experimental import pallas as pl
from jax.experimental.pallas import tpu as pltpu
from jax.sharding import PartitionSpec as P

F32 = jnp.float32
BF16 = jnp.bfloat16
I32 = jnp.int32
MIB = 1024 * 1024
VMEM = pltpu.VMEM
SMEM = pltpu.SMEM
UNROLL = 4
VMEM_LIMIT = 62 * MIB


def cost(microseconds):
    return pl.CostEstimate(flops=int(microseconds * 1e9), bytes_accessed=1000, transcendentals=0)


PARTS = 4
COSTS = dict(plan=2.0, u=1.0, early=(2.8, 2.5), late=2.5, pack=0.5)


def split(x):
    hi = x.astype(BF16)
    return hi, (x - hi.astype(F32)).astype(BF16)


def wide(x):
    hi, lo = split(x)
    return jnp.concatenate([hi, lo], axis=-1)


def tall(x):
    both = wide(x)
    return jnp.concatenate([both, both], axis=-2)


def fold(product):
    half = product.shape[-1] // 2
    return product[..., :half] + product[..., half:]


def dot(left, right):
    return jnp.dot(left, right, preferred_element_type=F32)


def dot_t(left, right):
    stacked = jnp.concatenate(split(left), axis=0)
    return fold(
        lax.dot_general(stacked, tall(right), (((0,), (0,)), ((), ())), preferred_element_type=F32)
    )


class Plan:
    def __init__(self, nodes, pieces, rows):
        entries = nodes * pieces
        self.parts = PARTS
        self.place = 0
        self.cls = self.place + entries
        self.slot = self.cls + entries
        self.node = self.slot + nodes * 2 * rows
        self.bounds = self.node + nodes
        self.ranges = 4 * self.parts + 1
        self.items = self.bounds + self.ranges * (rows - 1)
        self.span = entries + 1
        self.spare = self.items + self.span * (rows - 1)
        self.size = self.spare + 1


def plan_kernel(dims, plan, where, table, chip_of, struct, token, out):
    del token
    nodes, pieces, rows, cols, n_col = dims
    row, col = where[0], where[1]
    core = lax.rem(row, 2)
    per_set = nodes // 4
    near = cols // rows

    def clear(index, carry):
        out[plan.slot + index] = -1
        return carry

    lax.fori_loop(0, nodes * 2 * rows, clear, 0)

    def locate(kk, carry):
        side = jnp.where(kk >= nodes // 2, 1 - core, core)
        n = 2 * chip_of[lax.rem(kk, nodes // 2)] + side
        out[plan.node + kk] = n
        origin = (row - core + side) * pieces
        for j in range(pieces):
            block = struct[n, table[origin + j]]
            owner = lax.div(block, cols)
            shift = owner - col
            shift = jnp.where(shift < 0, shift + n_col, shift)
            group = lax.div(block, rows)
            out[plan.place + n * pieces + j] = (shift - owner) * near + group
            out[plan.cls + n * pieces + j] = block - group * rows
            for w in range(2):
                home = row if w == 0 else row + 1 - 2 * core
                spot = plan.slot + (n * 2 + w) * rows + block - home * rows
                out[jnp.where(group == home, spot, plan.spare)] = j
        return carry

    lax.fori_loop(0, nodes, locate, 0)
    for c in range(rows - 1):
        base = plan.items + plan.span * c
        bounds = plan.bounds + plan.ranges * c
        out[bounds] = 0

        def gather(a, count):
            ids, wants = [], []
            for t in range(per_set):
                n = out[plan.node + a * per_set + t]
                top = out[plan.slot + n * 2 * rows + c + 1]
                for i in range(c + 2, rows):
                    top = jnp.maximum(top, out[plan.slot + n * 2 * rows + i])
                ids.append(n * pieces)
                wants.append(top >= 0)
            for j in range(pieces):
                for t in range(per_set):
                    far = out[plan.place + ids[t] + j] >= near
                    wanted = far & (out[plan.cls + ids[t] + j] == c) & wants[t]
                    out[base + count] = (a * pieces + j) * per_set + t
                    count = count + jnp.where(wanted, 1, 0)
                if (j + 1) % (pieces // plan.parts) == 0:
                    out[bounds + a * plan.parts + (j + 1) // (pieces // plan.parts)] = count
            return count

        lax.fori_loop(0, 4, gather, jnp.int32(0))


def make_plan(plan, dims, where, table, chip_of, struct, token):
    smem = pl.BlockSpec(memory_space=SMEM)
    return pl.pallas_call(
        functools.partial(plan_kernel, dims, plan),
        out_shape=jax.ShapeDtypeStruct((plan.size,), I32),
        in_specs=[smem] * 4 + [pl.BlockSpec(memory_space=pl.ANY)],
        out_specs=smem,
        cost_estimate=cost(COSTS["plan"]),
        name="plan",
    )(where, table, chip_of, struct, token)


def u_kernel(chips, where, own, partner, inverse, out, square_out, f_buf, d_buf, u_buf, square, sems):
    core = lax.rem(where[0], 2)
    count = len(chips)
    loads = []
    for index, chip in enumerate(chips):
        n = 2 * chip + core
        loads.append(
            [
                pltpu.make_async_copy(inverse.at[n], d_buf.at[index], sems.at[0, index]),
                pltpu.make_async_copy(own.at[n], f_buf.at[0, index], sems.at[1, index]),
                pltpu.make_async_copy(partner.at[n], f_buf.at[1, index], sems.at[2, index]),
            ]
        )
    last = pltpu.make_async_copy(inverse.at[where[0]], d_buf.at[count], sems.at[0, count])
    for copies in loads:
        for copy in copies:
            copy.start()
    last.start()
    for index in range(count):
        for copy in loads[index]:
            copy.wait()
        right = tall(d_buf[index])
        for side in range(2):
            u_buf[side, index] = fold(dot(wide(f_buf[side, index]), right))
    stores = [pltpu.make_async_copy(u_buf, out, sems.at[1, count])]
    stores[0].start()
    last.wait()
    square[0] = dot_t(d_buf[count], d_buf[count])
    stores.append(pltpu.make_async_copy(square, square_out, sems.at[2, count]))
    stores[1].start()
    for copy in stores:
        copy.wait()


def u_blocks(chips, where, own, partner, inverse):
    count = len(chips)
    block = inverse.shape[1:]
    any_spec = pl.BlockSpec(memory_space=pl.ANY)
    return pl.pallas_call(
        functools.partial(u_kernel, chips),
        out_shape=[jax.ShapeDtypeStruct((2, count) + block, F32), jax.ShapeDtypeStruct((1,) + block, F32)],
        in_specs=[pl.BlockSpec(memory_space=SMEM)] + [any_spec] * 3,
        out_specs=[any_spec] * 2,
        scratch_shapes=[
            pltpu.VMEM((2, count) + block, F32),
            pltpu.VMEM((count + 1,) + block, F32),
            pltpu.VMEM((2, count) + block, F32),
            pltpu.VMEM((1,) + block, F32),
            pltpu.SemaphoreType.DMA((3, count + 1)),
        ],
        compiler_params=pltpu.CompilerParams(vmem_limit_bytes=VMEM_LIMIT),
        cost_estimate=cost(COSTS["u"]),
        name="u_blocks",
    )(where, own, partner, inverse)


def pack_kernel(pairs, groups, out, buf, sems):
    loads = [pltpu.make_async_copy(groups.at[i, :, c], buf.at[k], sems.at[0, k]) for k, (i, c) in enumerate(pairs)]
    stores = [pltpu.make_async_copy(buf.at[k], out.at[k], sems.at[1, k]) for k in range(len(pairs))]
    for copy in loads:
        copy.start()
    for load, store in zip(loads, stores):
        load.wait()
        store.start()
    for copy in stores:
        copy.wait()


def pack(pairs, groups):
    any_spec = pl.BlockSpec(memory_space=pl.ANY)
    shape = (len(pairs), groups.shape[1]) + groups.shape[3:]
    return pl.pallas_call(
        functools.partial(pack_kernel, pairs),
        out_shape=jax.ShapeDtypeStruct(shape, F32),
        in_specs=[any_spec],
        out_specs=any_spec,
        scratch_shapes=[pltpu.VMEM(shape, F32), pltpu.SemaphoreType.DMA((2, len(pairs)))],
        compiler_params=pltpu.CompilerParams(vmem_limit_bytes=VMEM_LIMIT),
        cost_estimate=cost(COSTS["pack"]),
        name="pack",
    )(groups)


def early_kernel(dims, plan, where, tables, *refs):
    rows, pieces, start, depth, chunk_z, zs = dims
    pairs = [(i, c) for i in range(rows) for c in range(i, rows)]
    near_refs, refs = refs[:2], refs[2:]
    far_refs, refs = refs[:2], refs[2:]
    hops = pieces // 2
    arrays, refs = refs[: hops + 1], refs[hops + 1 :]
    if start > 0:
        p_before, refs = refs[0], refs[1:]
    y_own, y_part, p_out, u_outs, refs = refs[0], refs[1], refs[2], refs[3 : 3 + plan.parts], refs[3 + plan.parts :]
    u_buf, u_wide, buf, acc, y_buf, p_buf, sems = refs
    count, width = y_own.shape[0], p_out.shape[-1]
    near = near_refs[0].shape[1]

    u_loads = []
    for k in range(hops + 1):
        for side in (0, 1) if k < hops - 1 else (k - hops + 1,):
            j = side * hops + min(k, hops - 1)
            source = arrays[k].at[side if k < hops - 1 else 0]
            u_loads.append((j, pltpu.make_async_copy(source, u_buf.at[j], sems.at[j])))
    for _, copy in u_loads:
        copy.start()

    def row_loads(k):
        w, i = divmod(k, rows)
        at = k % depth
        base = pieces + at * (1 + rows)
        loads = [pltpu.make_async_copy(near_refs[w].at[i], buf.at[at, pl.ds(0, near)], sems.at[base])]
        far = pl.ds(near, buf.shape[1] - near)
        for c in range(i, rows):
            source = far_refs[w].at[pairs.index((i, c))]
            loads.append(pltpu.make_async_copy(source, buf.at[at, far, c], sems.at[base + 1 + c]))
        return loads

    for k in range(min(depth, 2 * rows)):
        for copy in row_loads(k):
            copy.start()
    my_x = lax.rem(lax.div(where[0], 2), 2)
    my_z = lax.div(where[0], 4)

    def spot(z, x):
        return jnp.where(my_x == x, 0, zs) + lax.rem(z - my_z + zs, zs)

    spots = [spot(z, x) for z in chunk_z[1 if start > 0 else 0] for x in range(2)]
    if start > 0:
        from_before = [
            pltpu.make_async_copy(p_before.at[t], p_buf.at[spot(z, x)], sems.at[pieces + depth * (1 + rows) + t])
            for t, (z, x) in enumerate((z, x) for z in chunk_z[0] for x in range(2))
        ]
        for copy in from_before:
            copy.start()
    else:
        spots = list(range(count))
    for t in spots:
        p_buf[t] = jnp.zeros((width, width), F32)
    for j, copy in u_loads:
        copy.wait()

        def widen(t, carry):
            u_wide[j, t] = wide(u_buf[j, t])
            return carry

        lax.fori_loop(0, count, widen, 0)
    share = pieces // plan.parts
    u_backs = [
        pltpu.make_async_copy(u_buf.at[pl.ds(part * share, share)], u_out, sems.at[part])
        for part, u_out in enumerate(u_outs)
    ]
    for copy in u_backs:
        copy.start()
    for k in range(2 * rows):
        w, i = divmod(k, rows)
        at = k % depth
        for copy in row_loads(k):
            copy.wait()

        def node(local, carry):
            n = tables[plan.node + start + local]
            t = local
            if start > 0:
                t = spots[-1]
                for index in range(count - 1):
                    t = jnp.where(local == index, spots[index], t)
            slot = tables[plan.slot + n * 2 * rows + k]

            @pl.when(slot >= 0)
            def member():
                acc[...] = jnp.zeros_like(acc)
                for j in range(pieces):
                    place = tables[plan.place + n * pieces + j]
                    c = tables[plan.cls + n * pieces + j]
                    block = buf[at, place, c]
                    if i > 0:
                        block = jnp.where((place < near) | (c >= i), block, 0.0)
                    right = u_wide[j, local]
                    acc[c] += fold(dot(wide(block), jnp.concatenate([right, right], axis=0)))
                parts = [acc[c] for c in range(rows)]
                y_buf[w, local, i] = sum(parts[1:], parts[0])
                later = parts[i]
                for c in range(i + 1, rows):
                    later = later + 2.0 * parts[c]
                p_buf[t] += dot_t(u_buf[slot, local], later)

            return carry

        lax.fori_loop(0, count, node, 0)
        if k + depth < 2 * rows:
            for copy in row_loads(k + depth):
                copy.start()
    for t in spots:
        total = p_buf[t]
        p_buf[t] = 0.5 * (total + total.T)
    if start > 0:
        for copy in from_before:
            copy.wait()
    backs = [
        pltpu.make_async_copy(p_buf, p_out, sems.at[plan.parts]),
        pltpu.make_async_copy(y_buf.at[0], y_own, sems.at[plan.parts + 1]),
        pltpu.make_async_copy(y_buf.at[1], y_part, sems.at[plan.parts + 2]),
    ]
    for copy in backs:
        copy.start()
    for copy in u_backs + backs:
        copy.wait()


def early_sums(plan, where, tables, nears, fars, arrays, p_before, window, chunk_z, zs):
    _, count, width, _ = arrays[0].shape
    pieces = 2 * (len(arrays) - 1)
    rows = nears[0].shape[0]
    depth = 3
    start = 0 if p_before is None else p_before.shape[0]
    any_spec = pl.BlockSpec(memory_space=pl.ANY)
    smem = pl.BlockSpec(memory_space=SMEM)
    y_shape = jax.ShapeDtypeStruct((count, rows, width, width), F32)
    operands = [*nears, *fars, *arrays] + ([] if p_before is None else [p_before])
    return pl.pallas_call(
        functools.partial(early_kernel, (rows, pieces, start, depth, chunk_z, zs), plan),
        in_specs=[smem, smem] + [any_spec] * len(operands),
        out_specs=[any_spec] * (3 + plan.parts),
        scratch_shapes=[
            pltpu.VMEM((pieces, count, width, width), F32),
            pltpu.VMEM((pieces, count, width, 2 * width), BF16),
            pltpu.VMEM((depth, window // rows, rows, width, width), F32),
            pltpu.VMEM((rows, width, width), F32),
            pltpu.VMEM((2, count, rows, width, width), F32),
            pltpu.VMEM((start + count, width, width), F32),
            pltpu.SemaphoreType.DMA((pieces + depth * (1 + rows) + start,)),
        ],
        out_shape=[y_shape, y_shape, jax.ShapeDtypeStruct((start + count, width, width), F32)]
        + [jax.ShapeDtypeStruct((pieces // plan.parts, count, width, width), F32)] * plan.parts,
        compiler_params=pltpu.CompilerParams(vmem_limit_bytes=VMEM_LIMIT),
        cost_estimate=cost(COSTS["early"][1 if start > 0 else 0]),
        name="early_sums",
    )(where, tables, *operands)


def late_kernel(dims, plan, tables, late, *refs):
    rows, near, pieces, pairs = dims
    arrays, refs = refs[: 4 * plan.parts], refs[4 * plan.parts :]
    y_sets, (out, z, u_buf, sems) = refs[:4], refs[4:]
    width = z.shape[-1]
    per_set = z.shape[0] // 4
    share = pieces // plan.parts

    def node_of(kk):
        return tables[plan.node + kk]

    def u_copy(array, index, item):
        piece = lax.rem(lax.div(item, per_set), share)
        return pltpu.make_async_copy(array.at[piece, lax.rem(item, per_set)], u_buf.at[index], sems.at[0])

    begins, totals = [], []
    begin = jnp.int32(0)
    for c in range(rows - 1):
        bounds = plan.bounds + plan.ranges * c
        items = plan.items + plan.span * c
        for k in range(4 * plan.parts):

            def fetch(index, carry):
                u_copy(arrays[k], begin + index, tables[items + index]).start()
                return carry

            lax.fori_loop(tables[bounds + k], tables[bounds + k + 1], fetch, 0)
        begins.append(begin)
        totals.append(tables[bounds + plan.ranges - 1])
        begin = begin + totals[c]
    copies = [
        pltpu.make_async_copy(y_sets[a].at[t], z.at[node_of(a * per_set + t)], sems.at[1])
        for a in range(4)
        for t in range(per_set)
    ]
    for copy in copies:
        copy.start()
    for copy in copies:
        copy.wait()

    def arrive(index, carry):
        u_copy(arrays[0], index, 0).wait()
        return carry

    lax.fori_loop(0, begin, arrive, 0)
    for c in range(rows - 1):
        items = plan.items + plan.span * c
        span = range(c + 1, rows)

        def work(step, carry):
            products = []
            for v in range(UNROLL):
                index = step * UNROLL + v
                valid = index < totals[c]
                index = jnp.minimum(index, totals[c] - 1)
                item = tables[items + index]
                pair = lax.div(item, per_set)
                n = node_of(lax.div(pair, pieces) * per_set + lax.rem(item, per_set))
                place = tables[plan.place + n * pieces + lax.rem(pair, pieces)] - near
                left = jnp.concatenate([late[pairs.index((i, c)), place] for i in span], axis=0)
                left = jnp.where(valid, left, 0.0)
                products.append((n, fold(dot(wide(left), tall(u_buf[begins[c] + index])))))
            for n, product in products:
                for k, i in enumerate(span):
                    z[n, i] += product[k * width : (k + 1) * width]
            return carry

        lax.fori_loop(0, lax.div(totals[c] + UNROLL - 1, UNROLL), work, 0)

    def finish(n, carry):
        for i in range(rows):
            z[n, i] = jnp.where(tables[plan.slot + n * 2 * rows + i] >= 0, -z[n, i], 0.0)
        return carry

    lax.fori_loop(0, z.shape[0], finish, 0)
    back = pltpu.make_async_copy(z, out, sems.at[1])
    back.start()
    back.wait()


def late_sums(plan, tables, late, arrays, y_sets, shape, near, pieces, pairs):
    any_spec = pl.BlockSpec(memory_space=pl.ANY)
    operands = [*arrays, *y_sets]
    return pl.pallas_call(
        functools.partial(late_kernel, (shape[1], near, pieces, pairs), plan),
        in_specs=[pl.BlockSpec(memory_space=SMEM), pl.BlockSpec(memory_space=VMEM)] + [any_spec] * len(operands),
        out_specs=any_spec,
        out_shape=jax.ShapeDtypeStruct(shape, F32),
        scratch_shapes=[
            pltpu.VMEM(shape, F32),
            pltpu.VMEM((shape[0] * pieces,) + shape[2:], F32),
            pltpu.SemaphoreType.DMA((2,)),
        ],
        compiler_params=pltpu.CompilerParams(vmem_limit_bytes=VMEM_LIMIT),
        cost_estimate=cost(COSTS["late"]),
        name="late_sums",
    )(tables, late, *operands)


def ring_order(chips):
    return list(range(0, chips, 2)) + list(range(1, chips, 2))[::-1]


def body(n_row, n_col, sigma, factor, diag_inv, struct):
    rows, cols, width, _ = sigma.shape
    nodes = diag_inv.shape[0]
    window = cols * n_col
    chips = n_row // 2
    order = ring_order(chips)
    zs = chips // 2
    row = lax.axis_index("row")
    col = lax.axis_index("col")
    permute = lax.ppermute
    where = jnp.stack([row, col]).astype(I32)

    def pairs(step):
        return [(order[i] * 2 + c, order[(i + step) % chips] * 2 + c) for i in range(chips) for c in range(2)]

    swap_core = [(r, r ^ 1) for r in range(n_row)]
    swap_x = [(r, r ^ 2) for r in range(n_row)]
    full_hops = (chips - 1) // 2

    table = np.zeros((n_row, n_row), np.int32)
    for r in range(n_row):
        p = order.index(r // 2)
        hops = [0] + [-h for h in range(1, full_hops + 1)] + list(range(1, full_hops + 1)) + [chips // 2]
        for w in range(2):
            for j, h in enumerate(hops):
                table[r, w * chips + j] = 2 * order[(p + h) % chips] + ((r % 2) ^ w)
    pieces = n_row

    chunk_z = [[0, zs - 1], list(range(1, zs - 1))]
    chunks = [[2 * z + x for z in zz for x in range(2)] for zz in chunk_z]
    chip_of = np.asarray(sum(chunks, []), np.int32)

    def swapped(array):
        return permute(array, "row", swap_core)

    def tie(values, *tokens):
        return lax.optimization_barrier((*values, *tokens))[: len(values)]

    groups = sigma.reshape(rows, cols // rows, rows, width, width)
    early_pairs = [(i, c) for i in range(rows) for c in range(i, rows)]
    late_pairs = [(i, c) for i in range(1, rows) for c in range(i)]

    def over_col(source):
        got = [permute(source, "col", [((c + d) % n_col, c) for c in range(n_col)]) for d in range(1, n_col)]
        return got[0] if len(got) == 1 else jnp.concatenate(got, axis=1)

    own_factor = factor[0]
    part_factor = swapped(own_factor)
    far_own = over_col(pack(early_pairs, groups))
    near_part = swapped(sigma)
    u_own = []
    for chunk in chunks:
        u, square = u_blocks(chunk, where, own_factor, part_factor, diag_inv)
        u_own.append(u)
    moved = [[(u, u)] for u in u_own]
    plan = Plan(nodes, pieces, rows)
    tables = None
    for hop in range(full_hops + 1):
        for k in range(2):
            front = tie(moved[k][hop])
            if hop == 2 and k == 0:
                front = tie(front, tables)
            if hop == full_hops:
                front = (front[0][:1], front[1][1:])
            moved[k].append((permute(front[0], "row", pairs(1)), permute(front[1], "row", pairs(-1))))
        if hop == 0:
            tables = make_plan(
                plan, (nodes, pieces, rows, cols, n_col), where, table.reshape(-1), chip_of, struct, moved[0][1][0]
            )
    gathered = [
        [u_own[k]] + [r for r, _ in moved[k][1:-1]] + [l for _, l in moved[k][1:-1]] + list(moved[k][-1])
        for k in range(2)
    ]
    (far_own,) = tie((far_own,), *moved[0][-2], *moved[1][-2])
    far_part = swapped(far_own)
    late = over_col(pack(late_pairs, groups))

    y_own, y_part, u_all, u_part, p_sum = [], [], [], [], None
    for arrays in gathered:
        y_a, y_b, p_sum, *u_parts = early_sums(
            plan,
            where,
            tables,
            (groups, near_part.reshape(groups.shape)),
            (far_own, far_part),
            arrays,
            p_sum,
            window,
            chunk_z,
            zs,
        )
        y_own.append(y_a)
        y_part.append(swapped(y_b))
        u_all += u_parts
        u_part += [swapped(u) for u in u_parts]

    part_sum = p_sum[:zs] + permute(p_sum[zs:], "row", swap_x)
    z_diag = square + part_sum[:1]
    for m in range(1, zs):
        links = [(r, (r + 4 * m) % n_row) for r in range(n_row)]
        z_diag = z_diag + permute(part_sum[m : m + 1], "row", links)

    shape = (nodes, rows, width, width)
    z_off = late_sums(
        plan, tables, late, u_all + u_part, y_own + y_part, shape, cols // rows, pieces, late_pairs
    )
    return z_off, z_diag


def solution(mesh):
    in_specs = (
        P("row", "col", None, None),
        P("row", "col", None, None),
        P("col", None, None),
        P("col", None),
    )
    out_specs = (P("col", "row", None, None), P(("col", "row"), None, None))
    run = functools.partial(body, mesh.shape["row"], mesh.shape["col"])
    return jax.shard_map(run, mesh=mesh, in_specs=in_specs, out_specs=out_specs, check_vma=False)
```

```python
import functools

import jax
import jax.numpy as jnp
import numpy as np
from jax import lax
from jax.experimental import pallas as pl
from jax.experimental.pallas import tpu as pltpu
from jax.sharding import PartitionSpec as P

F32 = jnp.float32
BF16 = jnp.bfloat16
I32 = jnp.int32
MIB = 1024 * 1024
VMEM = pltpu.VMEM
SMEM = pltpu.SMEM
VMEM_LIMIT = 62 * MIB


def cost(microseconds):
    return pl.CostEstimate(flops=int(microseconds * 1e9), bytes_accessed=1000, transcendentals=0)


COSTS = dict(plan=1.0, u=1.0, sums=3.0)


def split(x):
    hi = x.astype(BF16)
    return hi, (x - hi.astype(F32)).astype(BF16)


def wide(x):
    hi, lo = split(x)
    return jnp.concatenate([hi, lo], axis=-1)


def tall(x):
    both = wide(x)
    return jnp.concatenate([both, both], axis=-2)


def fold(product):
    half = product.shape[-1] // 2
    return product[..., :half] + product[..., half:]


def dot(left, right):
    return jnp.dot(left, right, preferred_element_type=F32)


def dot_t(left, right):
    stacked = jnp.concatenate(split(left), axis=0)
    return fold(
        lax.dot_general(stacked, tall(right), (((0,), (0,)), ((), ())), preferred_element_type=F32)
    )


class Plan:
    def __init__(self, nodes, pieces, rows):
        self.place = 0
        self.slot = self.place + nodes * pieces
        self.node = self.slot + nodes * rows
        self.spare = self.node + nodes
        self.size = self.spare + 1


def plan_kernel(dims, plan, where, table, chip_of, struct, token, out):
    del token
    nodes, pieces, rows, cols, n_col = dims
    row, col = where[0], where[1]
    core = lax.rem(row, 2)

    def clear(index, carry):
        out[plan.slot + index] = -1
        return carry

    lax.fori_loop(0, nodes * rows, clear, 0)

    def locate(kk, carry):
        side = jnp.where(kk >= nodes // 2, 1 - core, core)
        n = 2 * chip_of[lax.rem(kk, nodes // 2)] + side
        origin = (row - core + side) * pieces
        out[plan.node + kk] = n
        for j in range(pieces):
            block = struct[n, table[origin + j]]
            shift = lax.div(block, cols) - col
            out[plan.place + kk * pieces + j] = block + jnp.where(shift < 0, n_col - col, -col) * cols
            first = block - row * rows
            inside = (first >= 0) & (first < rows)
            out[jnp.where(inside, plan.slot + kk * rows + first, plan.spare)] = j
        return carry

    lax.fori_loop(0, nodes, locate, 0)


def make_plan(plan, dims, where, table, chip_of, struct, token):
    smem = pl.BlockSpec(memory_space=SMEM)
    return pl.pallas_call(
        functools.partial(plan_kernel, dims, plan),
        out_shape=jax.ShapeDtypeStruct((plan.size,), I32),
        in_specs=[smem] * 4 + [pl.BlockSpec(memory_space=pl.ANY)],
        out_specs=smem,
        cost_estimate=cost(COSTS["plan"]),
        name="plan",
    )(where, table, chip_of, struct, token)


def u_kernel(chips, other, where, own, partner, inverse, token, out, square_out, f_buf, d_buf, u_buf, square, sems):
    del token
    core = lax.rem(where[0], 2)
    count = len(chips)
    loads = []
    for index, chip in enumerate(chips):
        n = 2 * chip + (1 - core if other else core)
        loads.append(
            [
                pltpu.make_async_copy(inverse.at[n], d_buf.at[index], sems.at[0, index]),
                pltpu.make_async_copy(own.at[n], f_buf.at[1 if other else 0, index], sems.at[1, index]),
                pltpu.make_async_copy(partner.at[n], f_buf.at[0 if other else 1, index], sems.at[2, index]),
            ]
        )
    last = pltpu.make_async_copy(inverse.at[where[0]], d_buf.at[count], sems.at[0, count])
    for copies in loads:
        for copy in copies:
            copy.start()
    last.start()
    for index in range(count):
        for copy in loads[index]:
            copy.wait()
        right = tall(d_buf[index])
        for side in range(2):
            u_buf[side, index] = fold(dot(wide(f_buf[side, index]), right))
    stores = [pltpu.make_async_copy(u_buf, out, sems.at[1, count])]
    stores[0].start()
    last.wait()
    square[0] = dot_t(d_buf[count], d_buf[count])
    stores.append(pltpu.make_async_copy(square, square_out, sems.at[2, count]))
    stores[1].start()
    for copy in stores:
        copy.wait()


def u_blocks(chips, other, where, own, partner, inverse, token):
    count = len(chips)
    block = inverse.shape[1:]
    any_spec = pl.BlockSpec(memory_space=pl.ANY)
    return pl.pallas_call(
        functools.partial(u_kernel, chips, other),
        out_shape=[jax.ShapeDtypeStruct((2, count) + block, F32), jax.ShapeDtypeStruct((1,) + block, F32)],
        in_specs=[pl.BlockSpec(memory_space=SMEM)] + [any_spec] * 4,
        out_specs=[any_spec] * 2,
        scratch_shapes=[
            pltpu.VMEM((2, count) + block, F32),
            pltpu.VMEM((count + 1,) + block, F32),
            pltpu.VMEM((2, count) + block, F32),
            pltpu.VMEM((1,) + block, F32),
            pltpu.SemaphoreType.DMA((3, count + 1)),
        ],
        compiler_params=pltpu.CompilerParams(vmem_limit_bytes=VMEM_LIMIT),
        cost_estimate=cost(COSTS["u"]),
        name="u_blocks",
    )(where, own, partner, inverse, token)


def sums_kernel(dims, plan, where, tables, near, far, *refs):
    rows, zs, chip_of, sets, hops = dims
    arrays, refs = refs[: sets * hops], refs[sets * hops :]
    z_out, p_outs, (u_buf, buf, z_buf, p_buf, sems) = refs[0], refs[1:4], refs[4:]
    per_set = u_buf.shape[2]
    pieces = u_buf.shape[1]
    width = u_buf.shape[-1]
    cols = near.shape[1]
    my_x = lax.rem(lax.div(where[0], 2), 2)
    my_z = lax.div(where[0], 4)
    sigma_loads = [
        pltpu.make_async_copy(near, buf.at[:, pl.ds(0, cols)], sems.at[0]),
        pltpu.make_async_copy(far, buf.at[:, pl.ds(cols, far.shape[1])], sems.at[1]),
    ]
    u_loads = [
        [
            pltpu.make_async_copy(arrays[a * hops + h].at[s], u_buf.at[a, s * hops + h], sems.at[2 + a])
            for h in range(hops)
            for s in range(2)
        ]
        for a in range(sets)
    ]
    for copies in [u_loads[0], sigma_loads] + u_loads[1:]:
        for copy in copies:
            copy.start()
    p_buf[...] = jnp.zeros_like(p_buf)

    def slot_of(kk, i):
        return tables[plan.slot + kk * rows + i]

    def products(kk, a, t, chosen):
        spots = [p_buf.shape[0] // 2 * (a // 2) + zs, p_buf.shape[0] // 2 * (a // 2)]
        chip = chip_of[0]
        at = (a % 2) * per_set + t
        for index in range(1, len(chip_of)):
            chip = jnp.where(at == index, chip_of[index], chip)
        spot = jnp.where(lax.rem(chip, 2) == my_x, spots[1], spots[0]) + lax.rem(lax.div(chip, 2) - my_z + zs, zs)
        y = jnp.zeros((len(chosen) * width, 2 * width), F32)
        for j in range(pieces):
            place = tables[plan.place + kk * pieces + j]
            left = jnp.concatenate([buf[i, place] for i in chosen], axis=0)
            y = y + dot(wide(left), tall(u_buf[a, j, t]))
        y = fold(y)
        for k, i in enumerate(chosen):
            part = y[k * width : (k + 1) * width]
            z_buf[kk, i] = -part
            p_buf[spot] += dot_t(u_buf[a, slot_of(kk, i), t], part)

    def node(kk, a, t):
        count = jnp.int32(0)
        for i in range(rows):
            count += jnp.where(slot_of(kk, i) >= 0, 1, 0)
        for i in range(rows):

            @pl.when(slot_of(kk, i) < 0)
            def absent():
                z_buf[kk, i] = jnp.zeros((width, width), F32)

        first = jnp.int32(rows - 1)
        last = jnp.int32(0)
        for i in range(rows):
            here = slot_of(kk, i) >= 0
            last = jnp.where(here, i, last)
            first = jnp.where(here, jnp.minimum(first, i), first)

        @pl.when(count == 1)
        def single():
            products(kk, a, t, [first])

        @pl.when(count == 2)
        def double():
            products(kk, a, t, [first, last])

        @pl.when(count >= 3)
        def several():
            products(kk, a, t, list(range(rows)))

    stores = []
    for a in range(sets):
        for copy in u_loads[a] + (sigma_loads if a == 0 else []):
            copy.wait()

        def step(t, carry):
            node(a * per_set + t, a, t)
            return carry

        lax.fori_loop(0, per_set, step, 0)
        for t in range(per_set):
            kk = a * per_set + t
            stores.append(pltpu.make_async_copy(z_buf.at[kk], z_out.at[tables[plan.node + kk]], sems.at[2 + sets]))
            stores[-1].start()
    for k, p_out in enumerate(p_outs):
        size = zs if k < 2 else 2 * zs
        stores.append(pltpu.make_async_copy(p_buf.at[pl.ds(k * zs, size)], p_out, sems.at[3 + sets + k]))
        stores[-1].start()
    for copy in stores:
        copy.wait()


def all_sums(plan, where, tables, near, far, u_sets, chip_of, zs):
    _, per_set, width, _ = u_sets[0][0].shape
    sets, hops = len(u_sets), len(u_sets[0])
    pieces = 2 * hops
    rows, cols = near.shape[:2]
    nodes = sets * per_set
    any_spec = pl.BlockSpec(memory_space=pl.ANY)
    smem = pl.BlockSpec(memory_space=SMEM)
    operands = [near, far] + [u for arrays in u_sets for u in arrays]
    shapes = [(nodes, rows), (zs,), (zs,), (2 * zs,)]
    return pl.pallas_call(
        functools.partial(sums_kernel, (rows, zs, chip_of, sets, hops), plan),
        in_specs=[smem, smem] + [any_spec] * len(operands),
        out_specs=[any_spec] * len(shapes),
        out_shape=[jax.ShapeDtypeStruct(shape + (width, width), F32) for shape in shapes],
        scratch_shapes=[
            pltpu.VMEM((sets, pieces, per_set, width, width), F32),
            pltpu.VMEM((rows, cols + far.shape[1], width, width), F32),
            pltpu.VMEM((nodes, rows, width, width), F32),
            pltpu.VMEM((4 * zs, width, width), F32),
            pltpu.SemaphoreType.DMA((6 + sets,)),
        ],
        compiler_params=pltpu.CompilerParams(vmem_limit_bytes=VMEM_LIMIT),
        cost_estimate=cost(COSTS["sums"]),
        name="all_sums",
    )(where, tables, *operands)


def ring_order(chips):
    return list(range(0, chips, 2)) + list(range(1, chips, 2))[::-1]


def body(n_row, n_col, sigma, factor, diag_inv, struct):
    rows, cols, width, _ = sigma.shape
    nodes = diag_inv.shape[0]
    window = cols * n_col
    chips = n_row // 2
    order = ring_order(chips)
    zs = chips // 2
    row = lax.axis_index("row")
    col = lax.axis_index("col")
    permute = lax.ppermute
    where = jnp.stack([row, col]).astype(I32)

    def pairs(step):
        return [(order[i] * 2 + c, order[(i + step) % chips] * 2 + c) for i in range(chips) for c in range(2)]

    swap_core = [(r, r ^ 1) for r in range(n_row)]
    swap_x = [(r, r ^ 2) for r in range(n_row)]
    full_hops = (chips - 1) // 2

    table = np.zeros((n_row, n_row), np.int32)
    for r in range(n_row):
        p = order.index(r // 2)
        hops = [0] + [-h for h in range(1, full_hops + 1)] + list(range(1, full_hops + 1)) + [chips // 2]
        for w in range(2):
            for j, h in enumerate(hops):
                table[r, w * chips + j] = 2 * order[(p + h) % chips] + ((r % 2) ^ w)
    pieces = n_row

    chunk_z = [[0, zs - 1], list(range(1, zs - 1))]
    chunks = [[2 * z + x for z in zz for x in range(2)] for zz in chunk_z]
    chip_of = sum(chunks, [])

    def swapped(array):
        return permute(array, "row", swap_core)

    def tie(values, *tokens):
        return lax.optimization_barrier((*values, *tokens))[: len(values)]

    def over_col(source):
        got = [permute(source, "col", [((c + d) % n_col, c) for c in range(n_col)]) for d in range(1, n_col)]
        return got[0] if len(got) == 1 else jnp.concatenate(got, axis=1)

    own_factor = factor[0]
    part_factor = swapped(own_factor)
    far = over_col(sigma)
    u_own = []
    for chunk in chunks:
        u, square = u_blocks(chunk, False, where, own_factor, part_factor, diag_inv, struct)
        u_own.append(u)
    moved = [[(u, u)] for u in u_own]
    plan = Plan(nodes, pieces, rows)
    tables = None
    for hop in range(full_hops + 1):
        for k in range(2):
            front = tie(moved[k][hop])
            if hop == 2 and k == 0:
                front = tie(front, tables)
            if hop == full_hops and k == 0:
                front = tie(front, *u_other)
            ways = ((1, -1) if hop < full_hops else (1,) if k == 0 else (-1,))
            moved[k].append(tuple(permute(front[0 if way > 0 else 1], "row", pairs(way)) for way in ways))
        if hop == 1:
            u_other = [
                u_blocks(chunk, True, where, own_factor, part_factor, diag_inv, moved[0][2][0])[0] for chunk in chunks
            ]
        if hop == 0:
            tables = make_plan(
                plan, (nodes, pieces, rows, cols, n_col), where, table.reshape(-1), np.asarray(chip_of, np.int32), struct, moved[0][1][0]
            )
    gathered = [
        [u_own[k]] + [r for r, _ in moved[k][1:-1]] + [l for _, l in moved[k][1:-1]] + list(moved[k][-1])
        for k in range(2)
    ]
    for k in range(2):
        pieces_here = tie(tuple(gathered[k][1:]), *moved[k][-1])
        gathered.append([u_other[k]] + [swapped(u) for u in pieces_here])
    z_off, mine, across, theirs = all_sums(plan, where, tables, sigma, far, gathered, chip_of, zs)

    got = swapped(theirs)
    part_sum = (mine + got[:zs]) + permute(across + got[zs:], "row", swap_x)
    z_diag = square + part_sum[:1]
    for m in range(1, zs):
        links = [(r, (r + 4 * m) % n_row) for r in range(n_row)]
        z_diag = z_diag + permute(part_sum[m : m + 1], "row", links)
    return z_off, z_diag


def solution(mesh):
    in_specs = (
        P("row", "col", None, None),
        P("row", "col", None, None),
        P("col", None, None),
        P("col", None),
    )
    out_specs = (P("col", "row", None, None), P(("col", "row"), None, None))
    run = functools.partial(body, mesh.shape["row"], mesh.shape["col"])
    return jax.shard_map(run, mesh=mesh, in_specs=in_specs, out_specs=out_specs, check_vma=False)
```

```python
import functools

import jax
import jax.numpy as jnp
import numpy as np
from jax import lax
from jax.experimental import pallas as pl
from jax.experimental.pallas import tpu as pltpu
from jax.sharding import PartitionSpec as P

F32 = jnp.float32
BF16 = jnp.bfloat16
I32 = jnp.int32
MIB = 1024 * 1024
VMEM = pltpu.VMEM
SMEM = pltpu.SMEM
VMEM_LIMIT = 62 * MIB


def cost(microseconds):
    return pl.CostEstimate(flops=int(microseconds * 1e9), bytes_accessed=1000, transcendentals=0)


COSTS = dict(plan=1.0, u=1.0, sums=3.0)


def split(x):
    hi = x.astype(BF16)
    return hi, (x - hi.astype(F32)).astype(BF16)


def wide(x):
    hi, lo = split(x)
    return jnp.concatenate([hi, lo], axis=-1)


def tall(x):
    both = wide(x)
    return jnp.concatenate([both, both], axis=-2)


def fold(product):
    half = product.shape[-1] // 2
    return product[..., :half] + product[..., half:]


def dot(left, right):
    return jnp.dot(left, right, preferred_element_type=F32)


def dot_t(left, right):
    stacked = jnp.concatenate(split(left), axis=0)
    return fold(
        lax.dot_general(stacked, tall(right), (((0,), (0,)), ((), ())), preferred_element_type=F32)
    )


class Plan:
    def __init__(self, nodes, pieces, rows):
        self.place = 0
        self.slot = self.place + nodes * pieces
        self.node = self.slot + nodes * rows
        self.spare = self.node + nodes
        self.size = self.spare + 1


def plan_kernel(dims, plan, where, table, chip_of, struct, token, out):
    del token
    nodes, pieces, rows, cols, n_col = dims
    row, col = where[0], where[1]
    core = lax.rem(row, 2)

    def clear(index, carry):
        out[plan.slot + index] = -1
        return carry

    lax.fori_loop(0, nodes * rows, clear, 0)

    def locate(kk, carry):
        side = jnp.where(kk >= nodes // 2, 1 - core, core)
        n = 2 * chip_of[lax.rem(kk, nodes // 2)] + side
        origin = (row - core + side) * pieces
        out[plan.node + kk] = n
        for j in range(pieces):
            block = struct[n, table[origin + j]]
            shift = lax.div(block, cols) - col
            out[plan.place + kk * pieces + j] = block + jnp.where(shift < 0, n_col - col, -col) * cols
            first = block - row * rows
            inside = (first >= 0) & (first < rows)
            out[jnp.where(inside, plan.slot + kk * rows + first, plan.spare)] = j
        return carry

    lax.fori_loop(0, nodes, locate, 0)


def make_plan(plan, dims, where, table, chip_of, struct, token):
    smem = pl.BlockSpec(memory_space=SMEM)
    return pl.pallas_call(
        functools.partial(plan_kernel, dims, plan),
        out_shape=jax.ShapeDtypeStruct((plan.size,), I32),
        in_specs=[smem] * 4 + [pl.BlockSpec(memory_space=pl.ANY)],
        out_specs=smem,
        cost_estimate=cost(COSTS["plan"]),
        name="plan",
    )(where, table, chip_of, struct, token)


def u_kernel(chips, other, where, own, partner, inverse, token, out, square_out, f_buf, d_buf, u_buf, square, sems):
    del token
    core = lax.rem(where[0], 2)
    count = len(chips)
    loads = []
    for index, chip in enumerate(chips):
        n = 2 * chip + (1 - core if other else core)
        loads.append(
            [
                pltpu.make_async_copy(inverse.at[n], d_buf.at[index], sems.at[0, index]),
                pltpu.make_async_copy(own.at[n], f_buf.at[1 if other else 0, index], sems.at[1, index]),
                pltpu.make_async_copy(partner.at[n], f_buf.at[0 if other else 1, index], sems.at[2, index]),
            ]
        )
    last = pltpu.make_async_copy(inverse.at[where[0]], d_buf.at[count], sems.at[0, count])
    for copies in loads:
        for copy in copies:
            copy.start()
    last.start()
    for index in range(count):
        for copy in loads[index]:
            copy.wait()
        right = tall(d_buf[index])
        for side in range(2):
            u_buf[side, index] = fold(dot(wide(f_buf[side, index]), right))
    stores = [pltpu.make_async_copy(u_buf, out, sems.at[1, count])]
    stores[0].start()
    last.wait()
    square[0] = dot_t(d_buf[count], d_buf[count])
    stores.append(pltpu.make_async_copy(square, square_out, sems.at[2, count]))
    stores[1].start()
    for copy in stores:
        copy.wait()


def u_blocks(chips, other, where, own, partner, inverse, token):
    count = len(chips)
    block = inverse.shape[1:]
    any_spec = pl.BlockSpec(memory_space=pl.ANY)
    return pl.pallas_call(
        functools.partial(u_kernel, chips, other),
        out_shape=[jax.ShapeDtypeStruct((2, count) + block, F32), jax.ShapeDtypeStruct((1,) + block, F32)],
        in_specs=[pl.BlockSpec(memory_space=SMEM)] + [any_spec] * 4,
        out_specs=[any_spec] * 2,
        scratch_shapes=[
            pltpu.VMEM((2, count) + block, F32),
            pltpu.VMEM((count + 1,) + block, F32),
            pltpu.VMEM((2, count) + block, F32),
            pltpu.VMEM((1,) + block, F32),
            pltpu.SemaphoreType.DMA((3, count + 1)),
        ],
        compiler_params=pltpu.CompilerParams(vmem_limit_bytes=VMEM_LIMIT),
        cost_estimate=cost(COSTS["u"]),
        name="u_blocks",
    )(where, own, partner, inverse, token)


def sums_kernel(dims, plan, where, tables, near, far, *refs):
    rows, zs, chip_of, sets, hops = dims
    arrays, refs = refs[: sets * hops], refs[sets * hops :]
    z_out, p_outs, (u_buf, buf, z_buf, p_buf, sems) = refs[0], refs[1:4], refs[4:]
    per_set = u_buf.shape[2]
    pieces = u_buf.shape[1]
    width = u_buf.shape[-1]
    cols = near.shape[1]
    my_x = lax.rem(lax.div(where[0], 2), 2)
    my_z = lax.div(where[0], 4)
    sigma_loads = [
        pltpu.make_async_copy(near, buf.at[:, pl.ds(0, cols)], sems.at[0]),
        pltpu.make_async_copy(far, buf.at[:, pl.ds(cols, far.shape[1])], sems.at[1]),
    ]
    u_loads = [
        [
            pltpu.make_async_copy(arrays[a * hops + h].at[s], u_buf.at[a, s * hops + h], sems.at[2 + a])
            for h in range(hops)
            for s in range(2)
        ]
        for a in range(sets)
    ]
    first_loads = [
        [
            pltpu.make_async_copy(arrays[h].at[s, t], u_buf.at[0, s * hops + h, t], sems.at[6 + sets + t])
            for h in range(hops)
            for s in range(2)
        ]
        for t in range(per_set)
    ]
    for copies in [sigma_loads] + first_loads + u_loads[1:]:
        for copy in copies:
            copy.start()

    def slot_of(kk, i):
        return tables[plan.slot + kk * rows + i]

    def products(kk, a, t, chosen):
        size = len(chosen) * width
        y = jnp.zeros((2 * size, 2 * width), F32)
        for j in range(0, pieces, 2):
            lefts, rights = [], []
            for slot in (j, j + 1):
                place = tables[plan.place + kk * pieces + slot]
                left = jnp.concatenate([buf[i, place] for i in chosen], axis=0)
                lefts.append(jnp.concatenate(split(left), axis=0))
                rights.append(wide(u_buf[a, slot, t]))
            y = y + dot(jnp.concatenate(lefts, axis=1), jnp.concatenate(rights, axis=0))
        y = fold(y[:size] + y[size:])
        for k, i in enumerate(chosen):
            z_buf[kk, i] = -y[k * width : (k + 1) * width]

    def diagonals(a):
        for t in range(per_set):
            kk = a * per_set + t
            own = len(chip_of)
            chip = jnp.int32(chip_of[0])
            for index in range(1, own):
                chip = jnp.where(lax.rem(kk, own) == index, chip_of[index], chip)
            spot = jnp.where(kk >= own, 2 * zs, 0) + jnp.where(lax.rem(chip, 2) == my_x, 0, zs)
            spot = spot + lax.rem(lax.div(chip, 2) - my_z + zs, zs)
            ups, downs = [], []
            for i in range(rows):
                slot = jnp.maximum(slot_of(kk, i), 0)
                ups.append(jnp.concatenate(split(u_buf[a, slot, t]), axis=0))
                downs.append(tall(z_buf[kk, i]))
            p_buf[spot] = -fold(
                lax.dot_general(
                    jnp.concatenate(ups, axis=0),
                    jnp.concatenate(downs, axis=0),
                    (((0,), (0,)), ((), ())),
                    preferred_element_type=F32,
                )
            )

    def node(kk, a, t):
        count = jnp.int32(0)
        for i in range(rows):
            count += jnp.where(slot_of(kk, i) >= 0, 1, 0)
        for i in range(rows):

            @pl.when(slot_of(kk, i) < 0)
            def absent():
                z_buf[kk, i] = jnp.zeros((width, width), F32)

        first = jnp.int32(rows - 1)
        last = jnp.int32(0)
        for i in range(rows):
            here = slot_of(kk, i) >= 0
            last = jnp.where(here, i, last)
            first = jnp.where(here, jnp.minimum(first, i), first)

        @pl.when(count == 1)
        def single():
            products(kk, a, t, [first])

        @pl.when(count == 2)
        def double():
            products(kk, a, t, [first, last])

        @pl.when(count >= 3)
        def several():
            products(kk, a, t, list(range(rows)))

    for copy in sigma_loads:
        copy.wait()

    def step(kk, carry):
        a, t = lax.div(kk, per_set), lax.rem(kk, per_set)

        @pl.when(a == 0)
        def arrive():
            def one(s, carry):
                pltpu.make_async_copy(arrays[0].at[0, 0], u_buf.at[0, s, t], sems.at[6 + sets + t]).wait()
                return carry

            lax.fori_loop(0, pieces, one, 0)

        for index in range(1, sets):

            @pl.when(kk == index * per_set)
            def arrive_set():
                for copy in u_loads[index]:
                    copy.wait()

        node(kk, a, t)

        @pl.when(t == per_set - 1)
        def close_set():
            diagonals(a)

        pltpu.make_async_copy(z_buf.at[kk], z_out.at[tables[plan.node + kk]], sems.at[2 + sets]).start()
        return carry

    lax.fori_loop(0, sets * per_set, step, 0)
    stores = []
    for k, p_out in enumerate(p_outs):
        size = zs if k < 2 else 2 * zs
        stores.append(pltpu.make_async_copy(p_buf.at[pl.ds(k * zs, size)], p_out, sems.at[3 + sets + k]))
        stores[-1].start()
    for copy in stores:
        copy.wait()

    def leave(kk, carry):
        pltpu.make_async_copy(z_buf.at[0], z_out.at[0], sems.at[2 + sets]).wait()
        return carry

    lax.fori_loop(0, sets * per_set, leave, 0)


def all_sums(plan, where, tables, near, far, u_sets, chip_of, zs):
    _, per_set, width, _ = u_sets[0][0].shape
    sets, hops = len(u_sets), len(u_sets[0])
    pieces = 2 * hops
    rows, cols = near.shape[:2]
    nodes = sets * per_set
    any_spec = pl.BlockSpec(memory_space=pl.ANY)
    smem = pl.BlockSpec(memory_space=SMEM)
    operands = [near, far] + [u for arrays in u_sets for u in arrays]
    shapes = [(nodes, rows), (zs,), (zs,), (2 * zs,)]
    return pl.pallas_call(
        functools.partial(sums_kernel, (rows, zs, chip_of, sets, hops), plan),
        in_specs=[smem, smem] + [any_spec] * len(operands),
        out_specs=[any_spec] * len(shapes),
        out_shape=[jax.ShapeDtypeStruct(shape + (width, width), F32) for shape in shapes],
        scratch_shapes=[
            pltpu.VMEM((sets, pieces, per_set, width, width), F32),
            pltpu.VMEM((rows, cols + far.shape[1], width, width), F32),
            pltpu.VMEM((nodes, rows, width, width), F32),
            pltpu.VMEM((4 * zs, width, width), F32),
            pltpu.SemaphoreType.DMA((6 + sets + per_set,)),
        ],
        compiler_params=pltpu.CompilerParams(vmem_limit_bytes=VMEM_LIMIT),
        cost_estimate=cost(COSTS["sums"]),
        name="all_sums",
    )(where, tables, *operands)


def ring_order(chips):
    return list(range(0, chips, 2)) + list(range(1, chips, 2))[::-1]


def body(n_row, n_col, sigma, factor, diag_inv, struct):
    rows, cols, width, _ = sigma.shape
    nodes = diag_inv.shape[0]
    window = cols * n_col
    chips = n_row // 2
    order = ring_order(chips)
    zs = chips // 2
    row = lax.axis_index("row")
    col = lax.axis_index("col")
    permute = lax.ppermute
    where = jnp.stack([row, col]).astype(I32)

    def pairs(step):
        return [(order[i] * 2 + c, order[(i + step) % chips] * 2 + c) for i in range(chips) for c in range(2)]

    swap_core = [(r, r ^ 1) for r in range(n_row)]
    swap_x = [(r, r ^ 2) for r in range(n_row)]
    full_hops = (chips - 1) // 2

    table = np.zeros((n_row, n_row), np.int32)
    for r in range(n_row):
        p = order.index(r // 2)
        hops = [0] + [-h for h in range(1, full_hops + 1)] + list(range(1, full_hops + 1)) + [chips // 2]
        for w in range(2):
            for j, h in enumerate(hops):
                table[r, w * chips + j] = 2 * order[(p + h) % chips] + ((r % 2) ^ w)
    pieces = n_row

    chunk_z = [[0, zs - 1], list(range(1, zs - 1))]
    chunks = [[2 * z + x for z in zz for x in range(2)] for zz in chunk_z]
    chip_of = sum(chunks, [])

    def swapped(array):
        return permute(array, "row", swap_core)

    def tie(values, *tokens):
        return lax.optimization_barrier((*values, *tokens))[: len(values)]

    def over_col(source):
        got = [permute(source, "col", [((c + d) % n_col, c) for c in range(n_col)]) for d in range(1, n_col)]
        return got[0] if len(got) == 1 else jnp.concatenate(got, axis=1)

    own_factor = factor[0]
    part_factor = swapped(own_factor)
    far = over_col(sigma)
    u_own = []
    for chunk in chunks:
        u, square = u_blocks(chunk, False, where, own_factor, part_factor, diag_inv, struct)
        u_own.append(u)
    moved = [[(u, u)] for u in u_own]
    plan = Plan(nodes, pieces, rows)
    tables = None
    for hop in range(full_hops + 1):
        for k in range(2):
            front = tie(moved[k][hop])
            if hop == 2 and k == 0:
                front = tie(front, tables)
            if hop == full_hops and k == 0:
                front = tie(front, *u_other)
            ways = ((1, -1) if hop < full_hops else (1,) if k == 0 else (-1,))
            moved[k].append(tuple(permute(front[0 if way > 0 else 1], "row", pairs(way)) for way in ways))
        if hop == 1:
            u_other = [
                u_blocks(chunk, True, where, own_factor, part_factor, diag_inv, moved[0][2][0])[0] for chunk in chunks
            ]
        if hop == 0:
            tables = make_plan(
                plan, (nodes, pieces, rows, cols, n_col), where, table.reshape(-1), np.asarray(chip_of, np.int32), struct, moved[0][1][0]
            )
    gathered = [
        [u_own[k]] + [r for r, _ in moved[k][1:-1]] + [l for _, l in moved[k][1:-1]] + list(moved[k][-1])
        for k in range(2)
    ]
    for k in range(2):
        pieces_here = tie(tuple(gathered[k][1:]), *moved[k][-1])
        gathered.append([u_other[k]] + [swapped(u) for u in pieces_here])
    z_off, mine, across, theirs = all_sums(plan, where, tables, sigma, far, gathered, chip_of, zs)

    got = swapped(theirs)
    here, there = mine + got[:zs], across + got[zs:]
    z_diag = square + here[:1]
    routes = [(m, flip) for flip in (1, 0) for m in range(zs) if m + flip > 0]
    for m, flip in routes:
        links = [(r, ((r + 4 * m) % n_row) ^ (2 * flip)) for r in range(n_row)]
        source = there if flip else here
        z_diag = z_diag + permute(source[m : m + 1], "row", links)
    return z_off, z_diag


def solution(mesh):
    in_specs = (
        P("row", "col", None, None),
        P("row", "col", None, None),
        P("col", None, None),
        P("col", None),
    )
    out_specs = (P("col", "row", None, None), P(("col", "row"), None, None))
    run = functools.partial(body, mesh.shape["row"], mesh.shape["col"])
    return jax.shard_map(run, mesh=mesh, in_specs=in_specs, out_specs=out_specs, check_vma=False)
```

```python
import functools

import jax
import jax.numpy as jnp
import numpy as np
from jax import lax
from jax.experimental import pallas as pl
from jax.experimental.pallas import tpu as pltpu
from jax.sharding import PartitionSpec as P

F32 = jnp.float32
BF16 = jnp.bfloat16
I32 = jnp.int32
MIB = 1024 * 1024
VMEM = pltpu.VMEM
SMEM = pltpu.SMEM
VMEM_LIMIT = 62 * MIB


def cost(microseconds):
    return pl.CostEstimate(flops=int(microseconds * 1e9), bytes_accessed=1000, transcendentals=0)


GROUP = 6
COSTS = dict(plan=1.0, u=1.0, sums=3.0)


def split(x):
    hi = x.astype(BF16)
    return hi, (x - hi.astype(F32)).astype(BF16)


def wide(x):
    hi, lo = split(x)
    return jnp.concatenate([hi, lo], axis=-1)


def tall(x):
    both = wide(x)
    return jnp.concatenate([both, both], axis=-2)


def fold(product):
    half = product.shape[-1] // 2
    return product[..., :half] + product[..., half:]


def dot(left, right):
    return jnp.dot(left, right, preferred_element_type=F32)


def dot_t(left, right):
    stacked = jnp.concatenate(split(left), axis=0)
    return fold(
        lax.dot_general(stacked, tall(right), (((0,), (0,)), ((), ())), preferred_element_type=F32)
    )


class Plan:
    def __init__(self, nodes, pieces, rows):
        self.place = 0
        self.slot = self.place + nodes * pieces
        self.node = self.slot + nodes * rows
        self.spare = self.node + nodes
        self.total = self.spare + 1
        self.items = self.total + 1
        self.size = self.items + nodes * rows + 1


def plan_kernel(dims, plan, where, table, chip_of, struct, token, out):
    del token
    nodes, pieces, rows, cols, n_col = dims
    row, col = where[0], where[1]
    core = lax.rem(row, 2)

    def clear(index, carry):
        out[plan.slot + index] = -1
        return carry

    lax.fori_loop(0, nodes * rows, clear, 0)

    def locate(kk, carry):
        side = jnp.where(kk >= nodes // 2, 1 - core, core)
        n = 2 * chip_of[lax.rem(kk, nodes // 2)] + side
        origin = (row - core + side) * pieces
        out[plan.node + kk] = n
        for j in range(pieces):
            block = struct[n, table[origin + j]]
            shift = lax.div(block, cols) - col
            out[plan.place + kk * pieces + j] = block + jnp.where(shift < 0, n_col - col, -col) * cols
            first = block - row * rows
            inside = (first >= 0) & (first < rows)
            out[jnp.where(inside, plan.slot + kk * rows + first, plan.spare)] = j
        return carry

    lax.fori_loop(0, nodes, locate, 0)

    def collect(kk, count):
        for i in range(rows):
            out[plan.items + count] = kk * rows + i
            count = count + jnp.where(out[plan.slot + kk * rows + i] >= 0, 1, 0)
        return count

    out[plan.total] = lax.fori_loop(0, nodes, collect, jnp.int32(0))


def make_plan(plan, dims, where, table, chip_of, struct, token):
    smem = pl.BlockSpec(memory_space=SMEM)
    return pl.pallas_call(
        functools.partial(plan_kernel, dims, plan),
        out_shape=jax.ShapeDtypeStruct((plan.size,), I32),
        in_specs=[smem] * 4 + [pl.BlockSpec(memory_space=pl.ANY)],
        out_specs=smem,
        cost_estimate=cost(COSTS["plan"]),
        name="plan",
    )(where, table, chip_of, struct, token)


def u_kernel(chips, other, where, own, partner, inverse, token, out, square_out, f_buf, d_buf, u_buf, square, sems):
    del token
    core = lax.rem(where[0], 2)
    count = len(chips)
    loads = []
    for index, chip in enumerate(chips):
        n = 2 * chip + (1 - core if other else core)
        loads.append(
            [
                pltpu.make_async_copy(inverse.at[n], d_buf.at[index], sems.at[0, index]),
                pltpu.make_async_copy(own.at[n], f_buf.at[1 if other else 0, index], sems.at[1, index]),
                pltpu.make_async_copy(partner.at[n], f_buf.at[0 if other else 1, index], sems.at[2, index]),
            ]
        )
    last = pltpu.make_async_copy(inverse.at[where[0]], d_buf.at[count], sems.at[0, count])
    for copies in loads:
        for copy in copies:
            copy.start()
    last.start()
    for index in range(count):
        for copy in loads[index]:
            copy.wait()
        right = tall(d_buf[index])
        for side in range(2):
            u_buf[side, index] = fold(dot(wide(f_buf[side, index]), right))
    stores = [pltpu.make_async_copy(u_buf, out, sems.at[1, count])]
    stores[0].start()
    last.wait()
    square[0] = dot_t(d_buf[count], d_buf[count])
    stores.append(pltpu.make_async_copy(square, square_out, sems.at[2, count]))
    stores[1].start()
    for copy in stores:
        copy.wait()


def u_blocks(chips, other, where, own, partner, inverse, token):
    count = len(chips)
    block = inverse.shape[1:]
    any_spec = pl.BlockSpec(memory_space=pl.ANY)
    return pl.pallas_call(
        functools.partial(u_kernel, chips, other),
        out_shape=[jax.ShapeDtypeStruct((2, count) + block, F32), jax.ShapeDtypeStruct((1,) + block, F32)],
        in_specs=[pl.BlockSpec(memory_space=SMEM)] + [any_spec] * 4,
        out_specs=[any_spec] * 2,
        scratch_shapes=[
            pltpu.VMEM((2, count) + block, F32),
            pltpu.VMEM((count + 1,) + block, F32),
            pltpu.VMEM((2, count) + block, F32),
            pltpu.VMEM((1,) + block, F32),
            pltpu.SemaphoreType.DMA((3, count + 1)),
        ],
        compiler_params=pltpu.CompilerParams(vmem_limit_bytes=VMEM_LIMIT),
        cost_estimate=cost(COSTS["u"]),
        name="u_blocks",
    )(where, own, partner, inverse, token)


def sums_kernel(dims, plan, where, tables, near, far, *refs):
    rows, zs, chip_of, sets, hops = dims
    arrays, refs = refs[: sets * hops], refs[sets * hops :]
    z_out, p_outs, (u_buf, buf, z_buf, p_buf, sems) = refs[0], refs[1:4], refs[4:]
    per_set = u_buf.shape[2]
    pieces = u_buf.shape[1]
    width = u_buf.shape[-1]
    cols = near.shape[1]
    my_x = lax.rem(lax.div(where[0], 2), 2)
    my_z = lax.div(where[0], 4)
    sigma_loads = [
        pltpu.make_async_copy(near, buf.at[:, pl.ds(0, cols)], sems.at[0]),
        pltpu.make_async_copy(far, buf.at[:, pl.ds(cols, far.shape[1])], sems.at[1]),
    ]
    u_loads = [
        [
            pltpu.make_async_copy(arrays[a * hops + h].at[s], u_buf.at[a, s * hops + h], sems.at[2 + a])
            for h in range(hops)
            for s in range(2)
        ]
        for a in range(sets)
    ]
    for copies in [sigma_loads] + u_loads:
        for copy in copies:
            copy.start()

    def clear(kk, carry):
        z_buf[kk] = jnp.zeros(z_buf.shape[1:], F32)
        return carry

    lax.fori_loop(0, z_buf.shape[0], clear, 0)

    def slot_of(kk, i):
        return tables[plan.slot + kk * rows + i]

    total = tables[plan.total]

    def item_of(index):
        item = tables[plan.items + jnp.minimum(index, total - 1)]
        return lax.div(item, rows), lax.rem(item, rows)

    def product(kk, i):
        a, t = lax.div(kk, per_set), lax.rem(kk, per_set)
        y = jnp.zeros((2 * width, 2 * width), F32)
        for j in range(0, pieces, 2):
            lefts, rights = [], []
            for slot in (j, j + 1):
                left = buf[i, tables[plan.place + kk * pieces + slot]]
                lefts.append(jnp.concatenate(split(left), axis=0))
                rights.append(wide(u_buf[a, slot, t]))
            y = y + dot(jnp.concatenate(lefts, axis=1), jnp.concatenate(rights, axis=0))
        return fold(y[:width] + y[width:])

    def diagonals(a):
        for t in range(per_set):
            kk = a * per_set + t
            own = len(chip_of)
            chip = jnp.int32(chip_of[0])
            for index in range(1, own):
                chip = jnp.where(lax.rem(kk, own) == index, chip_of[index], chip)
            spot = jnp.where(kk >= own, 2 * zs, 0) + jnp.where(lax.rem(chip, 2) == my_x, 0, zs)
            spot = spot + lax.rem(lax.div(chip, 2) - my_z + zs, zs)
            ups, downs = [], []
            for i in range(rows):
                slot = jnp.maximum(slot_of(kk, i), 0)
                ups.append(jnp.concatenate(split(u_buf[a, slot, t]), axis=0))
                downs.append(tall(z_buf[kk, i]))
            p_buf[spot] = -fold(
                lax.dot_general(
                    jnp.concatenate(ups, axis=0),
                    jnp.concatenate(downs, axis=0),
                    (((0,), (0,)), ((), ())),
                    preferred_element_type=F32,
                )
            )

    for copy in sigma_loads + u_loads[0]:
        copy.wait()

    def arrive(before, now):
        for a in range(1, sets):

            @pl.when((before < a) & (now >= a))
            def arrive_set():
                for copy in u_loads[a]:
                    copy.wait()

    def close(a, carry):
        diagonals(a)
        for t in range(per_set):
            kk = a * per_set + t
            pltpu.make_async_copy(z_buf.at[kk], z_out.at[tables[plan.node + kk]], sems.at[2 + sets]).start()
        return carry

    def step(group, carry):
        here, closed = carry
        found = [item_of(group * GROUP + k) for k in range(GROUP)]
        now = lax.div(found[-1][0], per_set)
        behind = lax.div(found[0][0], per_set)
        lax.fori_loop(closed, behind, close, 0)
        arrive(here, now)
        results = [product(kk, i) for kk, i in found]
        for (kk, i), y in zip(found, results):
            z_buf[kk, i] = -y
        return now, behind

    groups = lax.div(total + GROUP - 1, GROUP)
    here, closed = lax.fori_loop(0, groups, step, (jnp.int32(0), jnp.int32(0)))
    arrive(here, sets - 1)
    lax.fori_loop(closed, sets, close, 0)
    stores = []
    for k, p_out in enumerate(p_outs):
        size = zs if k < 2 else 2 * zs
        stores.append(pltpu.make_async_copy(p_buf.at[pl.ds(k * zs, size)], p_out, sems.at[3 + sets + k]))
        stores[-1].start()
    for copy in stores:
        copy.wait()

    def leave(kk, carry):
        pltpu.make_async_copy(z_buf.at[0], z_out.at[0], sems.at[2 + sets]).wait()
        return carry

    lax.fori_loop(0, sets * per_set, leave, 0)


def all_sums(plan, where, tables, near, far, u_sets, chip_of, zs):
    _, per_set, width, _ = u_sets[0][0].shape
    sets, hops = len(u_sets), len(u_sets[0])
    pieces = 2 * hops
    rows, cols = near.shape[:2]
    nodes = sets * per_set
    any_spec = pl.BlockSpec(memory_space=pl.ANY)
    smem = pl.BlockSpec(memory_space=SMEM)
    operands = [near, far] + [u for arrays in u_sets for u in arrays]
    shapes = [(nodes, rows), (zs,), (zs,), (2 * zs,)]
    return pl.pallas_call(
        functools.partial(sums_kernel, (rows, zs, chip_of, sets, hops), plan),
        in_specs=[smem, smem] + [any_spec] * len(operands),
        out_specs=[any_spec] * len(shapes),
        out_shape=[jax.ShapeDtypeStruct(shape + (width, width), F32) for shape in shapes],
        scratch_shapes=[
            pltpu.VMEM((sets, pieces, per_set, width, width), F32),
            pltpu.VMEM((rows, cols + far.shape[1], width, width), F32),
            pltpu.VMEM((nodes, rows, width, width), F32),
            pltpu.VMEM((4 * zs, width, width), F32),
            pltpu.SemaphoreType.DMA((6 + sets + per_set,)),
        ],
        compiler_params=pltpu.CompilerParams(vmem_limit_bytes=VMEM_LIMIT),
        cost_estimate=cost(COSTS["sums"]),
        name="all_sums",
    )(where, tables, *operands)


def ring_order(chips):
    return list(range(0, chips, 2)) + list(range(1, chips, 2))[::-1]


def body(n_row, n_col, sigma, factor, diag_inv, struct):
    rows, cols, width, _ = sigma.shape
    nodes = diag_inv.shape[0]
    window = cols * n_col
    chips = n_row // 2
    order = ring_order(chips)
    zs = chips // 2
    row = lax.axis_index("row")
    col = lax.axis_index("col")
    permute = lax.ppermute
    where = jnp.stack([row, col]).astype(I32)

    def pairs(step):
        return [(order[i] * 2 + c, order[(i + step) % chips] * 2 + c) for i in range(chips) for c in range(2)]

    swap_core = [(r, r ^ 1) for r in range(n_row)]
    swap_x = [(r, r ^ 2) for r in range(n_row)]
    full_hops = (chips - 1) // 2

    table = np.zeros((n_row, n_row), np.int32)
    for r in range(n_row):
        p = order.index(r // 2)
        hops = [0] + [-h for h in range(1, full_hops + 1)] + list(range(1, full_hops + 1)) + [chips // 2]
        for w in range(2):
            for j, h in enumerate(hops):
                table[r, w * chips + j] = 2 * order[(p + h) % chips] + ((r % 2) ^ w)
    pieces = n_row

    chunk_z = [[0, zs - 1], list(range(1, zs - 1))]
    chunks = [[2 * z + x for z in zz for x in range(2)] for zz in chunk_z]
    chip_of = sum(chunks, [])

    def swapped(array):
        return permute(array, "row", swap_core)

    def tie(values, *tokens):
        return lax.optimization_barrier((*values, *tokens))[: len(values)]

    def over_col(source):
        got = [permute(source, "col", [((c + d) % n_col, c) for c in range(n_col)]) for d in range(1, n_col)]
        return got[0] if len(got) == 1 else jnp.concatenate(got, axis=1)

    own_factor = factor[0]
    part_factor = swapped(own_factor)
    far = over_col(sigma)
    u_own = []
    for chunk in chunks:
        u, square = u_blocks(chunk, False, where, own_factor, part_factor, diag_inv, struct)
        u_own.append(u)
    moved = [[(u, u)] for u in u_own]
    plan = Plan(nodes, pieces, rows)
    tables = None
    for hop in range(full_hops + 1):
        for k in range(2):
            front = tie(moved[k][hop])
            if hop == 2 and k == 0:
                front = tie(front, tables)
            if hop == full_hops and k == 0:
                front = tie(front, *u_other)
            ways = ((1, -1) if hop < full_hops else (1,) if k == 0 else (-1,))
            moved[k].append(tuple(permute(front[0 if way > 0 else 1], "row", pairs(way)) for way in ways))
        if hop == 1:
            u_other = [
                u_blocks(chunk, True, where, own_factor, part_factor, diag_inv, moved[0][2][0])[0] for chunk in chunks
            ]
        if hop == 0:
            tables = make_plan(
                plan, (nodes, pieces, rows, cols, n_col), where, table.reshape(-1), np.asarray(chip_of, np.int32), struct, moved[0][1][0]
            )
    gathered = [
        [u_own[k]] + [r for r, _ in moved[k][1:-1]] + [l for _, l in moved[k][1:-1]] + list(moved[k][-1])
        for k in range(2)
    ]
    for k in range(2):
        pieces_here = tie(tuple(gathered[k][1:]), *moved[k][-1])
        gathered.append([u_other[k]] + [swapped(u) for u in pieces_here])
    z_off, mine, across, theirs = all_sums(plan, where, tables, sigma, far, gathered, chip_of, zs)

    got = swapped(theirs)
    here, there = mine + got[:zs], across + got[zs:]
    z_diag = square + here[:1]
    routes = [(m, flip) for flip in (1, 0) for m in range(zs) if m + flip > 0]
    for m, flip in routes:
        links = [(r, ((r + 4 * m) % n_row) ^ (2 * flip)) for r in range(n_row)]
        source = there if flip else here
        z_diag = z_diag + permute(source[m : m + 1], "row", links)
    return z_off, z_diag


def solution(mesh):
    in_specs = (
        P("row", "col", None, None),
        P("row", "col", None, None),
        P("col", None, None),
        P("col", None),
    )
    out_specs = (P("col", "row", None, None), P(("col", "row"), None, None))
    run = functools.partial(body, mesh.shape["row"], mesh.shape["col"])
    return jax.shard_map(run, mesh=mesh, in_specs=in_specs, out_specs=out_specs, check_vma=False)
```

```python
import functools

import jax
import jax.numpy as jnp
import numpy as np
from jax import lax
from jax.experimental import pallas as pl
from jax.experimental.pallas import tpu as pltpu
from jax.sharding import PartitionSpec as P

F32 = jnp.float32
BF16 = jnp.bfloat16
I32 = jnp.int32
MIB = 1024 * 1024
VMEM = pltpu.VMEM
SMEM = pltpu.SMEM
VMEM_LIMIT = 62 * MIB


def cost(microseconds):
    return pl.CostEstimate(flops=int(microseconds * 1e9), bytes_accessed=1000, transcendentals=0)


GROUP = 6
COSTS = dict(plan=1.0, u=1.0, sums=3.0)


def split(x):
    hi = x.astype(BF16)
    return hi, (x - hi.astype(F32)).astype(BF16)


def wide(x):
    hi, lo = split(x)
    return jnp.concatenate([hi, lo], axis=-1)


def tall(x):
    both = wide(x)
    return jnp.concatenate([both, both], axis=-2)


def fold(product):
    half = product.shape[-1] // 2
    return product[..., :half] + product[..., half:]


def dot(left, right):
    return jnp.dot(left, right, preferred_element_type=F32)


def dot_t(left, right):
    stacked = jnp.concatenate(split(left), axis=0)
    return fold(
        lax.dot_general(stacked, tall(right), (((0,), (0,)), ((), ())), preferred_element_type=F32)
    )


class Plan:
    def __init__(self, nodes, pieces, rows):
        self.place = 0
        self.slot = self.place + nodes * pieces
        self.node = self.slot + nodes * rows
        self.spare = self.node + nodes
        self.total = self.spare + 1
        self.items = self.total + 1
        self.size = self.items + nodes * rows + 1


def plan_kernel(dims, plan, where, table, chip_of, struct, token, out):
    del token
    nodes, pieces, rows, cols, n_col = dims
    row, col = where[0], where[1]
    core = lax.rem(row, 2)

    def clear(index, carry):
        out[plan.slot + index] = -1
        return carry

    lax.fori_loop(0, nodes * rows, clear, 0)

    def locate(kk, carry):
        side = jnp.where(kk >= nodes // 2, 1 - core, core)
        n = 2 * chip_of[lax.rem(kk, nodes // 2)] + side
        origin = (row - core + side) * pieces
        out[plan.node + kk] = n
        for j in range(pieces):
            block = struct[n, table[origin + j]]
            shift = lax.div(block, cols) - col
            out[plan.place + kk * pieces + j] = block + jnp.where(shift < 0, n_col - col, -col) * cols
            first = block - row * rows
            inside = (first >= 0) & (first < rows)
            out[jnp.where(inside, plan.slot + kk * rows + first, plan.spare)] = j
        return carry

    lax.fori_loop(0, nodes, locate, 0)

    def collect(kk, count):
        for i in range(rows):
            out[plan.items + count] = kk * rows + i
            count = count + jnp.where(out[plan.slot + kk * rows + i] >= 0, 1, 0)
        return count

    out[plan.total] = lax.fori_loop(0, nodes, collect, jnp.int32(0))


def make_plan(plan, dims, where, table, chip_of, struct, token):
    smem = pl.BlockSpec(memory_space=SMEM)
    return pl.pallas_call(
        functools.partial(plan_kernel, dims, plan),
        out_shape=jax.ShapeDtypeStruct((plan.size,), I32),
        in_specs=[smem] * 4 + [pl.BlockSpec(memory_space=pl.ANY)],
        out_specs=smem,
        cost_estimate=cost(COSTS["plan"]),
        name="plan",
    )(where, table, chip_of, struct, token)


def u_kernel(chips, other, where, own, partner, inverse, token, out, square_out, f_buf, d_buf, u_buf, square, sems):
    del token
    core = lax.rem(where[0], 2)
    count = len(chips)
    loads = []
    for index, chip in enumerate(chips):
        n = 2 * chip + (1 - core if other else core)
        loads.append(
            [
                pltpu.make_async_copy(inverse.at[n], d_buf.at[index], sems.at[0, index]),
                pltpu.make_async_copy(own.at[n], f_buf.at[1 if other else 0, index], sems.at[1, index]),
                pltpu.make_async_copy(partner.at[n], f_buf.at[0 if other else 1, index], sems.at[2, index]),
            ]
        )
    last = pltpu.make_async_copy(inverse.at[where[0]], d_buf.at[count], sems.at[0, count])
    for copies in loads:
        for copy in copies:
            copy.start()
    last.start()
    for index in range(count):
        for copy in loads[index]:
            copy.wait()
        right = tall(d_buf[index])
        for side in range(2):
            u_buf[side, index] = fold(dot(wide(f_buf[side, index]), right))
    stores = [pltpu.make_async_copy(u_buf, out, sems.at[1, count])]
    stores[0].start()
    last.wait()
    square[0] = dot_t(d_buf[count], d_buf[count])
    stores.append(pltpu.make_async_copy(square, square_out, sems.at[2, count]))
    stores[1].start()
    for copy in stores:
        copy.wait()


def u_blocks(chips, other, where, own, partner, inverse, token):
    count = len(chips)
    block = inverse.shape[1:]
    any_spec = pl.BlockSpec(memory_space=pl.ANY)
    return pl.pallas_call(
        functools.partial(u_kernel, chips, other),
        out_shape=[jax.ShapeDtypeStruct((2, count) + block, F32), jax.ShapeDtypeStruct((1,) + block, F32)],
        in_specs=[pl.BlockSpec(memory_space=SMEM)] + [any_spec] * 4,
        out_specs=[any_spec] * 2,
        scratch_shapes=[
            pltpu.VMEM((2, count) + block, F32),
            pltpu.VMEM((count + 1,) + block, F32),
            pltpu.VMEM((2, count) + block, F32),
            pltpu.VMEM((1,) + block, F32),
            pltpu.SemaphoreType.DMA((3, count + 1)),
        ],
        compiler_params=pltpu.CompilerParams(vmem_limit_bytes=VMEM_LIMIT),
        cost_estimate=cost(COSTS["u"]),
        name="u_blocks",
    )(where, own, partner, inverse, token)


def sums_kernel(dims, plan, where, tables, near, far, *refs):
    rows, zs, chip_of, sets, hops = dims
    arrays, refs = refs[: sets * hops], refs[sets * hops :]
    z_out, p_outs, (u_buf, buf, z_buf, p_buf, sems) = refs[0], refs[1:4], refs[4:]
    per_set = u_buf.shape[2]
    pieces = u_buf.shape[1]
    width = u_buf.shape[-1]
    cols = near.shape[1]
    my_x = lax.rem(lax.div(where[0], 2), 2)
    my_z = lax.div(where[0], 4)
    sigma_loads = [
        pltpu.make_async_copy(near, buf.at[:, pl.ds(0, cols)], sems.at[0]),
        pltpu.make_async_copy(far, buf.at[:, pl.ds(cols, far.shape[1])], sems.at[1]),
    ]
    u_loads = [
        [
            pltpu.make_async_copy(arrays[a * hops + h].at[s], u_buf.at[a, s * hops + h], sems.at[2 + a])
            for h in range(hops)
            for s in range(2)
        ]
        for a in range(sets)
    ]
    for copies in [sigma_loads] + u_loads:
        for copy in copies:
            copy.start()

    def clear(kk, carry):
        z_buf[kk] = jnp.zeros(z_buf.shape[1:], F32)
        return carry

    lax.fori_loop(0, z_buf.shape[0], clear, 0)

    def slot_of(kk, i):
        return tables[plan.slot + kk * rows + i]

    total = tables[plan.total]

    def item_of(index):
        item = tables[plan.items + jnp.minimum(index, total - 1)]
        return lax.div(item, rows), lax.rem(item, rows)

    def product(kk, i):
        a, t = lax.div(kk, per_set), lax.rem(kk, per_set)
        y = jnp.zeros((2 * width, 2 * width), F32)
        for j in range(0, pieces, 2):
            lefts, rights = [], []
            for slot in (j, j + 1):
                left = buf[i, tables[plan.place + kk * pieces + slot]]
                lefts.append(jnp.concatenate(split(left), axis=0))
                rights.append(wide(u_buf[a, slot, t]))
            y = y + dot(jnp.concatenate(lefts, axis=1), jnp.concatenate(rights, axis=0))
        return fold(y[:width] + y[width:])

    def diagonals(a):
        for t in range(per_set):
            kk = a * per_set + t
            own = len(chip_of)
            chip = jnp.int32(chip_of[0])
            for index in range(1, own):
                chip = jnp.where(lax.rem(kk, own) == index, chip_of[index], chip)
            spot = jnp.where(kk >= own, 2 * zs, 0) + jnp.where(lax.rem(chip, 2) == my_x, 0, zs)
            spot = spot + lax.rem(lax.div(chip, 2) - my_z + zs, zs)
            ups, downs = [], []
            for i in range(rows):
                slot = jnp.maximum(slot_of(kk, i), 0)
                ups.append(jnp.concatenate(split(u_buf[a, slot, t]), axis=0))
                downs.append(tall(z_buf[kk, i]))
            p_buf[spot] = -fold(
                lax.dot_general(
                    jnp.concatenate(ups, axis=0),
                    jnp.concatenate(downs, axis=0),
                    (((0,), (0,)), ((), ())),
                    preferred_element_type=F32,
                )
            )

    for copy in sigma_loads + u_loads[0]:
        copy.wait()

    def arrive(before, now):
        for a in range(1, sets):

            @pl.when((before < a) & (now >= a))
            def arrive_set():
                for copy in u_loads[a]:
                    copy.wait()

    def close(a, carry):
        diagonals(a)
        for t in range(per_set):
            kk = a * per_set + t
            pltpu.make_async_copy(z_buf.at[kk], z_out.at[tables[plan.node + kk]], sems.at[2 + sets]).start()
        return carry

    def step(group, carry):
        here, closed = carry
        found = [item_of(group * GROUP + k) for k in range(GROUP)]
        now = lax.div(found[-1][0], per_set)
        behind = lax.div(found[0][0], per_set)
        lax.fori_loop(closed, behind, close, 0)
        arrive(here, now)
        results = [product(kk, i) for kk, i in found]
        for (kk, i), y in zip(found, results):
            z_buf[kk, i] = -y
        return now, behind

    groups = lax.div(total + GROUP - 1, GROUP)
    here, closed = lax.fori_loop(0, groups, step, (jnp.int32(0), jnp.int32(0)))
    arrive(here, sets - 1)
    lax.fori_loop(closed, sets, close, 0)
    stores = []
    for k, p_out in enumerate(p_outs):
        size = zs if k < 2 else 2 * zs
        stores.append(pltpu.make_async_copy(p_buf.at[pl.ds(k * zs, size)], p_out, sems.at[3 + sets + k]))
        stores[-1].start()
    for copy in stores:
        copy.wait()

    def leave(kk, carry):
        pltpu.make_async_copy(z_buf.at[0], z_out.at[0], sems.at[2 + sets]).wait()
        return carry

    lax.fori_loop(0, sets * per_set, leave, 0)


def all_sums(plan, where, tables, near, far, u_sets, chip_of, zs):
    _, per_set, width, _ = u_sets[0][0].shape
    sets, hops = len(u_sets), len(u_sets[0])
    pieces = 2 * hops
    rows, cols = near.shape[:2]
    nodes = sets * per_set
    any_spec = pl.BlockSpec(memory_space=pl.ANY)
    smem = pl.BlockSpec(memory_space=SMEM)
    operands = [near, far] + [u for arrays in u_sets for u in arrays]
    shapes = [(nodes, rows), (zs,), (zs,), (2 * zs,)]
    return pl.pallas_call(
        functools.partial(sums_kernel, (rows, zs, chip_of, sets, hops), plan),
        in_specs=[smem, smem] + [any_spec] * len(operands),
        out_specs=[any_spec] * len(shapes),
        out_shape=[jax.ShapeDtypeStruct(shape + (width, width), F32) for shape in shapes],
        scratch_shapes=[
            pltpu.VMEM((sets, pieces, per_set, width, width), F32),
            pltpu.VMEM((rows, cols + far.shape[1], width, width), F32),
            pltpu.VMEM((nodes, rows, width, width), F32),
            pltpu.VMEM((4 * zs, width, width), F32),
            pltpu.SemaphoreType.DMA((6 + sets + per_set,)),
        ],
        compiler_params=pltpu.CompilerParams(vmem_limit_bytes=VMEM_LIMIT),
        cost_estimate=cost(COSTS["sums"]),
        name="all_sums",
    )(where, tables, *operands)


def ring_order(chips):
    return list(range(0, chips, 2)) + list(range(1, chips, 2))[::-1]


def body(n_row, n_col, sigma, factor, diag_inv, struct):
    rows, cols, width, _ = sigma.shape
    nodes = diag_inv.shape[0]
    window = cols * n_col
    chips = n_row // 2
    order = ring_order(chips)
    zs = chips // 2
    row = lax.axis_index("row")
    col = lax.axis_index("col")
    permute = lax.ppermute
    where = jnp.stack([row, col]).astype(I32)

    def pairs(step):
        return [(order[i] * 2 + c, order[(i + step) % chips] * 2 + c) for i in range(chips) for c in range(2)]

    swap_core = [(r, r ^ 1) for r in range(n_row)]
    swap_x = [(r, r ^ 2) for r in range(n_row)]
    full_hops = (chips - 1) // 2

    table = np.zeros((n_row, n_row), np.int32)
    for r in range(n_row):
        p = order.index(r // 2)
        hops = [0] + [-h for h in range(1, full_hops + 1)] + list(range(1, full_hops + 1)) + [chips // 2]
        for w in range(2):
            for j, h in enumerate(hops):
                table[r, w * chips + j] = 2 * order[(p + h) % chips] + ((r % 2) ^ w)
    pieces = n_row

    chunk_z = [[0, zs - 1], list(range(1, zs - 1))]
    chunks = [[2 * z + x for z in zz for x in range(2)] for zz in chunk_z]
    chip_of = sum(chunks, [])

    def swapped(array):
        return permute(array, "row", swap_core)

    def tie(values, *tokens):
        return lax.optimization_barrier((*values, *tokens))[: len(values)]

    def over_col(source):
        got = [permute(source, "col", [((c + d) % n_col, c) for c in range(n_col)]) for d in range(1, n_col)]
        return got[0] if len(got) == 1 else jnp.concatenate(got, axis=1)

    own_factor = factor[0]
    part_factor = swapped(own_factor)
    far = over_col(sigma)
    u_own = []
    for chunk in chunks:
        u, square = u_blocks(chunk, False, where, own_factor, part_factor, diag_inv, struct)
        u_own.append(u)
    moved = [[(u, u)] for u in u_own]
    plan = Plan(nodes, pieces, rows)
    tables = None
    for hop in range(full_hops + 1):
        for k in range(2):
            front = tie(moved[k][hop])
            if hop == 2 and k == 0:
                front = tie(front, tables)
            if hop == full_hops and k == 0:
                front = tie(front, *u_other)
            ways = ((1, -1) if hop < full_hops else (1,) if k == 0 else (-1,))
            moved[k].append(tuple(permute(front[0 if way > 0 else 1], "row", pairs(way)) for way in ways))
        if hop == 1:
            u_other = [
                u_blocks(chunk, True, where, own_factor, part_factor, diag_inv, moved[0][2][0])[0] for chunk in chunks
            ]
        if hop == 0:
            tables = make_plan(
                plan, (nodes, pieces, rows, cols, n_col), where, table.reshape(-1), np.asarray(chip_of, np.int32), struct, moved[0][1][0]
            )
    gathered = [
        [u_own[k]] + [r for r, _ in moved[k][1:-1]] + [l for _, l in moved[k][1:-1]] + list(moved[k][-1])
        for k in range(2)
    ]
    for k in range(2):
        pieces_here = tie(tuple(gathered[k][1:]), *moved[k][-1])
        gathered.append([u_other[k]] + [swapped(u) for u in pieces_here])
    z_off, mine, across, theirs = all_sums(plan, where, tables, sigma, far, gathered, chip_of, zs)

    got = swapped(theirs)
    here, there = mine + got[:zs], across + got[zs:]
    z_diag = square + here[:1]
    routes = sorted(((m, flip) for flip in (1, 0) for m in range(zs) if m + flip > 0), key=lambda r: min(r[0], zs - r[0]))
    for m, flip in routes:
        links = [(r, ((r + 4 * m) % n_row) ^ (2 * flip)) for r in range(n_row)]
        source = there if flip else here
        z_diag = z_diag + permute(source[m : m + 1], "row", links)
    return z_off, z_diag


def solution(mesh):
    in_specs = (
        P("row", "col", None, None),
        P("row", "col", None, None),
        P("col", None, None),
        P("col", None),
    )
    out_specs = (P("col", "row", None, None), P(("col", "row"), None, None))
    run = functools.partial(body, mesh.shape["row"], mesh.shape["col"])
    return jax.shard_map(run, mesh=mesh, in_specs=in_specs, out_specs=out_specs, check_vma=False)
```

```python
import functools

import jax
import jax.numpy as jnp
import numpy as np
from jax import lax
from jax.experimental import pallas as pl
from jax.experimental.pallas import tpu as pltpu
from jax.sharding import PartitionSpec as P

F32 = jnp.float32
BF16 = jnp.bfloat16
I32 = jnp.int32
MIB = 1024 * 1024
VMEM = pltpu.VMEM
SMEM = pltpu.SMEM
VMEM_LIMIT = 62 * MIB


def cost(microseconds):
    return pl.CostEstimate(flops=int(microseconds * 1e9), bytes_accessed=1000, transcendentals=0)


GROUP = 6
COSTS = dict(plan=1.0, u=1.0, sums=3.0)


def split(x):
    hi = x.astype(BF16)
    return hi, (x - hi.astype(F32)).astype(BF16)


def wide(x):
    hi, lo = split(x)
    return jnp.concatenate([hi, lo], axis=-1)


def tall(x):
    both = wide(x)
    return jnp.concatenate([both, both], axis=-2)


def fold(product):
    half = product.shape[-1] // 2
    return product[..., :half] + product[..., half:]


def dot(left, right):
    return jnp.dot(left, right, preferred_element_type=F32)


def dot_t(left, right):
    stacked = jnp.concatenate(split(left), axis=0)
    return fold(
        lax.dot_general(stacked, tall(right), (((0,), (0,)), ((), ())), preferred_element_type=F32)
    )


class Plan:
    def __init__(self, nodes, pieces, rows):
        self.place = 0
        self.slot = self.place + nodes * pieces
        self.node = self.slot + nodes * rows
        self.spare = self.node + nodes
        self.total = self.spare + 1
        self.items = self.total + 1
        self.size = self.items + nodes * rows + 1


def plan_kernel(dims, plan, where, table, chip_of, struct, token, out):
    del token
    nodes, pieces, rows, cols, n_col = dims
    row, col = where[0], where[1]
    core = lax.rem(row, 2)

    def clear(index, carry):
        out[plan.slot + index] = -1
        return carry

    lax.fori_loop(0, nodes * rows, clear, 0)

    def locate(kk, carry):
        side = jnp.where(kk >= nodes // 2, 1 - core, core)
        n = 2 * chip_of[lax.rem(kk, nodes // 2)] + side
        origin = (row - core + side) * pieces
        out[plan.node + kk] = n
        for j in range(pieces):
            block = struct[n, table[origin + j]]
            shift = lax.div(block, cols) - col
            out[plan.place + kk * pieces + j] = block + jnp.where(shift < 0, n_col - col, -col) * cols
            first = block - row * rows
            inside = (first >= 0) & (first < rows)
            out[jnp.where(inside, plan.slot + kk * rows + first, plan.spare)] = j
        return carry

    lax.fori_loop(0, nodes, locate, 0)

    def collect(kk, count):
        for i in range(rows):
            out[plan.items + count] = kk * rows + i
            count = count + jnp.where(out[plan.slot + kk * rows + i] >= 0, 1, 0)
        return count

    out[plan.total] = lax.fori_loop(0, nodes, collect, jnp.int32(0))


def make_plan(plan, dims, where, table, chip_of, struct, token):
    smem = pl.BlockSpec(memory_space=SMEM)
    return pl.pallas_call(
        functools.partial(plan_kernel, dims, plan),
        out_shape=jax.ShapeDtypeStruct((plan.size,), I32),
        in_specs=[smem] * 4 + [pl.BlockSpec(memory_space=pl.ANY)],
        out_specs=smem,
        cost_estimate=cost(COSTS["plan"]),
        name="plan",
    )(where, table, chip_of, struct, token)


def u_kernel(chips, other, where, own, partner, inverse, token, out, square_out, f_buf, d_buf, u_buf, square, sems):
    del token
    core = lax.rem(where[0], 2)
    count = len(chips)
    loads = []
    for index, chip in enumerate(chips):
        n = 2 * chip + (1 - core if other else core)
        loads.append(
            [
                pltpu.make_async_copy(inverse.at[n], d_buf.at[index], sems.at[0, index]),
                pltpu.make_async_copy(own.at[n], f_buf.at[1 if other else 0, index], sems.at[1, index]),
                pltpu.make_async_copy(partner.at[n], f_buf.at[0 if other else 1, index], sems.at[2, index]),
            ]
        )
    last = pltpu.make_async_copy(inverse.at[where[0]], d_buf.at[count], sems.at[0, count])
    for copies in loads:
        for copy in copies:
            copy.start()
    last.start()
    for index in range(count):
        for copy in loads[index]:
            copy.wait()
        right = tall(d_buf[index])
        for side in range(2):
            u_buf[side, index] = fold(dot(wide(f_buf[side, index]), right))
    stores = [pltpu.make_async_copy(u_buf, out, sems.at[1, count])]
    stores[0].start()
    last.wait()
    square[0] = dot_t(d_buf[count], d_buf[count])
    stores.append(pltpu.make_async_copy(square, square_out, sems.at[2, count]))
    stores[1].start()
    for copy in stores:
        copy.wait()


def u_blocks(chips, other, where, own, partner, inverse, token):
    count = len(chips)
    block = inverse.shape[1:]
    any_spec = pl.BlockSpec(memory_space=pl.ANY)
    return pl.pallas_call(
        functools.partial(u_kernel, chips, other),
        out_shape=[jax.ShapeDtypeStruct((2, count) + block, F32), jax.ShapeDtypeStruct((1,) + block, F32)],
        in_specs=[pl.BlockSpec(memory_space=SMEM)] + [any_spec] * 4,
        out_specs=[any_spec] * 2,
        scratch_shapes=[
            pltpu.VMEM((2, count) + block, F32),
            pltpu.VMEM((count + 1,) + block, F32),
            pltpu.VMEM((2, count) + block, F32),
            pltpu.VMEM((1,) + block, F32),
            pltpu.SemaphoreType.DMA((3, count + 1)),
        ],
        compiler_params=pltpu.CompilerParams(vmem_limit_bytes=VMEM_LIMIT),
        cost_estimate=cost(COSTS["u"]),
        name="u_blocks",
    )(where, own, partner, inverse, token)


def sums_kernel(dims, plan, where, tables, near, far, *refs):
    rows, zs, chip_of, sets, hops = dims
    arrays, refs = refs[: sets * hops], refs[sets * hops :]
    z_out, p_outs, (u_buf, buf, z_buf, p_buf, sems) = refs[0], refs[1:4], refs[4:]
    per_set = u_buf.shape[2]
    pieces = u_buf.shape[1]
    width = u_buf.shape[-1]
    cols = near.shape[1]
    my_x = lax.rem(lax.div(where[0], 2), 2)
    my_z = lax.div(where[0], 4)
    sigma_loads = [
        pltpu.make_async_copy(near, buf.at[:, pl.ds(0, cols)], sems.at[0]),
        pltpu.make_async_copy(far, buf.at[:, pl.ds(cols, far.shape[1])], sems.at[1]),
    ]
    u_loads = [
        [
            pltpu.make_async_copy(arrays[a * hops + h].at[s], u_buf.at[a, s * hops + h], sems.at[2 + a])
            for h in range(hops)
            for s in range(2)
        ]
        for a in range(sets)
    ]
    for copies in [sigma_loads] + u_loads:
        for copy in copies:
            copy.start()

    def clear(kk, carry):
        z_buf[kk] = jnp.zeros(z_buf.shape[1:], F32)
        return carry

    lax.fori_loop(0, z_buf.shape[0], clear, 0)

    def slot_of(kk, i):
        return tables[plan.slot + kk * rows + i]

    total = tables[plan.total]

    def item_of(index):
        item = tables[plan.items + jnp.minimum(index, total - 1)]
        return lax.div(item, rows), lax.rem(item, rows)

    def product(kk, i):
        a, t = lax.div(kk, per_set), lax.rem(kk, per_set)
        y = jnp.zeros((2 * width, 2 * width), F32)
        for j in range(0, pieces, 2):
            lefts, rights = [], []
            for slot in (j, j + 1):
                left = buf[i, tables[plan.place + kk * pieces + slot]]
                lefts.append(jnp.concatenate(split(left), axis=0))
                rights.append(wide(u_buf[a, slot, t]))
            y = y + dot(jnp.concatenate(lefts, axis=1), jnp.concatenate(rights, axis=0))
        return fold(y[:width] + y[width:])

    def diagonals(a):
        for t in range(per_set):
            kk = a * per_set + t
            own = len(chip_of)
            chip = jnp.int32(chip_of[0])
            for index in range(1, own):
                chip = jnp.where(lax.rem(kk, own) == index, chip_of[index], chip)
            spot = jnp.where(kk >= own, 2 * zs, 0) + jnp.where(lax.rem(chip, 2) == my_x, 0, zs)
            spot = spot + lax.rem(lax.div(chip, 2) - my_z + zs, zs)
            ups, downs = [], []
            for i in range(rows):
                slot = jnp.maximum(slot_of(kk, i), 0)
                ups.append(jnp.concatenate(split(u_buf[a, slot, t]), axis=0))
                downs.append(tall(z_buf[kk, i]))
            p_buf[spot] = -fold(
                lax.dot_general(
                    jnp.concatenate(ups, axis=0),
                    jnp.concatenate(downs, axis=0),
                    (((0,), (0,)), ((), ())),
                    preferred_element_type=F32,
                )
            )

    for copy in sigma_loads + u_loads[0]:
        copy.wait()

    def arrive(before, now):
        for a in range(1, sets):

            @pl.when((before < a) & (now >= a))
            def arrive_set():
                for copy in u_loads[a]:
                    copy.wait()

    def close(a, carry):
        for t in range(per_set):
            kk = a * per_set + t
            pltpu.make_async_copy(z_buf.at[kk], z_out.at[tables[plan.node + kk]], sems.at[2 + sets]).start()
        diagonals(a)
        return carry

    def step(group, carry):
        here, closed = carry
        found = [item_of(group * GROUP + k) for k in range(GROUP)]
        now = lax.div(found[-1][0], per_set)
        behind = lax.div(found[0][0], per_set)
        lax.fori_loop(closed, behind, close, 0)
        arrive(here, now)
        results = [product(kk, i) for kk, i in found]
        for (kk, i), y in zip(found, results):
            z_buf[kk, i] = -y
        return now, behind

    groups = lax.div(total + GROUP - 1, GROUP)
    here, closed = lax.fori_loop(0, groups, step, (jnp.int32(0), jnp.int32(0)))
    arrive(here, sets - 1)
    lax.fori_loop(closed, sets, close, 0)
    stores = []
    for k, p_out in enumerate(p_outs):
        size = zs if k < 2 else 2 * zs
        stores.append(pltpu.make_async_copy(p_buf.at[pl.ds(k * zs, size)], p_out, sems.at[3 + sets + k]))
        stores[-1].start()
    for copy in stores:
        copy.wait()

    def leave(kk, carry):
        pltpu.make_async_copy(z_buf.at[0], z_out.at[0], sems.at[2 + sets]).wait()
        return carry

    lax.fori_loop(0, sets * per_set, leave, 0)


def all_sums(plan, where, tables, near, far, u_sets, chip_of, zs):
    _, per_set, width, _ = u_sets[0][0].shape
    sets, hops = len(u_sets), len(u_sets[0])
    pieces = 2 * hops
    rows, cols = near.shape[:2]
    nodes = sets * per_set
    any_spec = pl.BlockSpec(memory_space=pl.ANY)
    smem = pl.BlockSpec(memory_space=SMEM)
    operands = [near, far] + [u for arrays in u_sets for u in arrays]
    shapes = [(nodes, rows), (zs,), (zs,), (2 * zs,)]
    return pl.pallas_call(
        functools.partial(sums_kernel, (rows, zs, chip_of, sets, hops), plan),
        in_specs=[smem, smem] + [any_spec] * len(operands),
        out_specs=[any_spec] * len(shapes),
        out_shape=[jax.ShapeDtypeStruct(shape + (width, width), F32) for shape in shapes],
        scratch_shapes=[
            pltpu.VMEM((sets, pieces, per_set, width, width), F32),
            pltpu.VMEM((rows, cols + far.shape[1], width, width), F32),
            pltpu.VMEM((nodes, rows, width, width), F32),
            pltpu.VMEM((4 * zs, width, width), F32),
            pltpu.SemaphoreType.DMA((6 + sets + per_set,)),
        ],
        compiler_params=pltpu.CompilerParams(vmem_limit_bytes=VMEM_LIMIT),
        cost_estimate=cost(COSTS["sums"]),
        name="all_sums",
    )(where, tables, *operands)


def ring_order(chips):
    return list(range(0, chips, 2)) + list(range(1, chips, 2))[::-1]


def body(n_row, n_col, sigma, factor, diag_inv, struct):
    rows, cols, width, _ = sigma.shape
    nodes = diag_inv.shape[0]
    window = cols * n_col
    chips = n_row // 2
    order = ring_order(chips)
    zs = chips // 2
    row = lax.axis_index("row")
    col = lax.axis_index("col")
    permute = lax.ppermute
    where = jnp.stack([row, col]).astype(I32)

    def pairs(step):
        return [(order[i] * 2 + c, order[(i + step) % chips] * 2 + c) for i in range(chips) for c in range(2)]

    swap_core = [(r, r ^ 1) for r in range(n_row)]
    swap_x = [(r, r ^ 2) for r in range(n_row)]
    full_hops = (chips - 1) // 2

    table = np.zeros((n_row, n_row), np.int32)
    for r in range(n_row):
        p = order.index(r // 2)
        hops = [0] + [-h for h in range(1, full_hops + 1)] + list(range(1, full_hops + 1)) + [chips // 2]
        for w in range(2):
            for j, h in enumerate(hops):
                table[r, w * chips + j] = 2 * order[(p + h) % chips] + ((r % 2) ^ w)
    pieces = n_row

    chunk_z = [[0, zs - 1], list(range(1, zs - 1))]
    chunks = [[2 * z + x for z in zz for x in range(2)] for zz in chunk_z]
    chip_of = sum(chunks, [])

    def swapped(array):
        return permute(array, "row", swap_core)

    def tie(values, *tokens):
        return lax.optimization_barrier((*values, *tokens))[: len(values)]

    def over_col(source):
        got = [permute(source, "col", [((c + d) % n_col, c) for c in range(n_col)]) for d in range(1, n_col)]
        return got[0] if len(got) == 1 else jnp.concatenate(got, axis=1)

    own_factor = factor[0]
    part_factor = swapped(own_factor)
    far = over_col(sigma)
    u_own = []
    for chunk in chunks:
        u, square = u_blocks(chunk, False, where, own_factor, part_factor, diag_inv, struct)
        u_own.append(u)
    moved = [[(u, u)] for u in u_own]
    plan = Plan(nodes, pieces, rows)
    tables = None
    for hop in range(full_hops + 1):
        for k in range(2):
            front = tie(moved[k][hop])
            if hop == 2 and k == 0:
                front = tie(front, tables)
            if hop == full_hops and k == 0:
                front = tie(front, *u_other)
            ways = ((1, -1) if hop < full_hops else (1,) if k == 0 else (-1,))
            moved[k].append(tuple(permute(front[0 if way > 0 else 1], "row", pairs(way)) for way in ways))
        if hop == 1:
            u_other = [
                u_blocks(chunk, True, where, own_factor, part_factor, diag_inv, moved[0][2][0])[0] for chunk in chunks
            ]
        if hop == 0:
            tables = make_plan(
                plan, (nodes, pieces, rows, cols, n_col), where, table.reshape(-1), np.asarray(chip_of, np.int32), struct, moved[0][1][0]
            )
    gathered = [
        [u_own[k]] + [r for r, _ in moved[k][1:-1]] + [l for _, l in moved[k][1:-1]] + list(moved[k][-1])
        for k in range(2)
    ]
    for k in range(2):
        pieces_here = tie(tuple(gathered[k][1:]), *moved[k][-1])
        gathered.append([u_other[k]] + [swapped(u) for u in pieces_here])
    z_off, mine, across, theirs = all_sums(plan, where, tables, sigma, far, gathered, chip_of, zs)

    got = swapped(theirs)
    here, there = mine + got[:zs], across + got[zs:]
    z_diag = square + here[:1]
    routes = sorted(((m, flip) for flip in (1, 0) for m in range(zs) if m + flip > 0), key=lambda r: min(r[0], zs - r[0]))
    for m, flip in routes:
        links = [(r, ((r + 4 * m) % n_row) ^ (2 * flip)) for r in range(n_row)]
        source = there if flip else here
        z_diag = z_diag + permute(source[m : m + 1], "row", links)
    return z_off, z_diag


def solution(mesh):
    in_specs = (
        P("row", "col", None, None),
        P("row", "col", None, None),
        P("col", None, None),
        P("col", None),
    )
    out_specs = (P("col", "row", None, None), P(("col", "row"), None, None))
    run = functools.partial(body, mesh.shape["row"], mesh.shape["col"])
    return jax.shard_map(run, mesh=mesh, in_specs=in_specs, out_specs=out_specs, check_vma=False)
```
